32 devices in a mesh: grp: 2 (over x), par: 16 (over z, y, core).
Axes of the slice: x: 2, y: 2, z: 4, core: 2. Of those that a mesh axis runs over, the one named last changes fastest.
Arguments:
- omega: bfloat16 [32, 131072], P(None, 'par'), may hold values from -6 to 6
- jac_blocks: bfloat16 [2, 2048, 128, 128], P('grp', 'par'), may hold values from -0.1796875 to 0.1796875
- block_param: int32 [2, 2048], P('grp', 'par'), may hold values from 0 to 63
- block_obs: int32 [2, 2048], P('grp', 'par'), may hold values from 0 to 63
- block_count: int32 [2, 16], P('grp', 'par'), may hold values from 16 to 128, as said below
- obs_weight: float32 [2, 8192], P('grp'), may hold values from 0.1 to 1
Outputs:
- hess_probe: float32 [32, 131072], P(None, ('par', 'grp'))
The draws below stay inside these ranges and needn't reach their ends.
Inputs may be any that keep to these rules, and one draw needn't show every extreme that they name: `block_count`: in every group four devices use all 128 slots and one device uses the fewest; the others use at most 64.
All inputs are finite; a program needn't handle non-finite values.
Results may differ from the reference program's by a relative error of at most 0.0027.
Values may be sent and summed in bfloat16 or wider, within the bound.
A program may use at most 64 MiB of HBM per device.

```python
import math
import jax
import jax.numpy as jnp
from jax import lax

K = 32
BLK = 128
PB = 64
CAP = 128
OB = 64
GROUPS = 2
NPAR = 131072
OBS = 8192
SLOTS = 2048
N_GRP = 2
N_PAR = 16


def draw_block_count(key, part):
    first = jax.random.fold_in(key, 11)
    second = jax.random.fold_in(key, 23)
    lower = max(1, CAP // 8)
    base = jax.random.randint(first, (N_GRP, N_PAR), lower, CAP // 2 + 1)
    scores = jax.random.randint(second, (N_GRP, N_PAR), 0, 1 << 20) * N_PAR + jnp.arange(N_PAR, dtype=jnp.int32)[None, :]
    ranks = jnp.argsort(jnp.argsort(scores, axis=1), axis=1)
    counts = jnp.where(ranks < 4, CAP, base)
    counts = jnp.where(ranks == 4, lower, counts)
    return counts.astype(jnp.int32)


def plant(values, stream_key, low, largest):
    longest = values.shape.index(max(values.shape))
    spots = []
    for shift in (0, 1):
        where = [jax.random.randint(jax.random.fold_in(stream_key, axis), (), 0, length) for axis, length in enumerate(values.shape)]
        where[longest] = (where[longest] + shift) % values.shape[longest]
        spots.append(tuple(where))
    return values.at[spots[0]].set(low).at[spots[1]].set(largest)


def block_scale(rng, extent, shards, smallest, largest):
    gain, own = 1.0, jax.random.fold_in(rng, 6)
    for axis_at, blocks in shards:
        steps = jnp.exp(jax.random.uniform(jax.random.fold_in(own, axis_at), (blocks,), jnp.float32, smallest / len(shards), largest / len(shards)))
        gain = gain * jnp.repeat(steps, extent[axis_at] // blocks).reshape([-1 if axis == axis_at else 1 for axis in range(len(extent))])
    return gain


def bell_draw(key, extent, spread, bound, split=(), held_as=jnp.bfloat16):
    array = spread * jax.random.normal(key, extent, jnp.float32)
    if split:
        array = array * block_scale(key, extent, split, -0.22, 0.18)
    return jnp.clip(array, -bound, bound).astype(held_as)


def setup_inputs(seed: int = 0) -> dict:
    seeds = jax.random.split(jax.random.key(seed), 7)
    omega = bell_draw(seeds[0], (K, NPAR), 1.0, 6.0, ((1, 16),))
    jac_blocks = bell_draw(seeds[1], (GROUPS, SLOTS, BLK, BLK), 0.03, 0.1796875, ((0, 2), (1, 16)))
    block_param = plant(jax.random.randint(seeds[2], (GROUPS, SLOTS), 0, PB), jax.random.fold_in(seeds[2], 1), 0, PB - 1).astype(jnp.int32)
    block_obs = plant(jax.random.randint(seeds[3], (GROUPS, SLOTS), 0, OB), jax.random.fold_in(seeds[3], 1), 0, OB - 1).astype(jnp.int32)
    block_count = draw_block_count(jax.random.fold_in(seeds[6], 71), 0)
    obs_weight = jnp.clip(jnp.exp(math.log(1.0) - 2.3025851 * jax.random.uniform(seeds[5], (GROUPS, OBS), jnp.float32) ** block_scale(seeds[5], (GROUPS, OBS), ((0, 2),), -0.2, 0.2)), 0.1, 1.0)
    return dict(omega=omega, jac_blocks=jac_blocks, block_param=block_param, block_obs=block_obs, block_count=block_count, obs_weight=obs_weight)


def reference(omega, jac_blocks, block_param, block_obs, block_count, obs_weight):
    n_par = N_PAR
    slots = CAP * n_par
    panels = omega.reshape(K, n_par * PB, BLK)
    shard = jnp.arange(slots, dtype=jnp.int32) // CAP
    within = jnp.arange(slots, dtype=jnp.int32) % CAP

    def one_group(total, inputs):
        blocks, bparam, bobs, counts, weights = inputs
        active = (within < counts[shard]).astype(jnp.float32)
        gidx = (shard * PB + bparam).astype(jnp.int32)
        picked = jnp.take(panels, gidx, axis=1).astype(jnp.float32)
        terms = jnp.einsum("kcp,cpo->cko", picked, blocks.astype(jnp.float32))
        terms = terms * active[:, None, None]
        fwd = jax.ops.segment_sum(terms, bobs, num_segments=OB)
        fwd = jnp.transpose(fwd, (1, 0, 2)).reshape(K, OB * BLK)
        scaled = (fwd * weights[None, :]).astype(jnp.bfloat16)
        vblocks = scaled.reshape(K, OB, BLK)
        pickv = jnp.take(vblocks, bobs, axis=1).astype(jnp.float32)
        back = jnp.einsum("kco,cpo->ckp", pickv, blocks.astype(jnp.float32))
        back = back * active[:, None, None]
        summed = jax.ops.segment_sum(back, gidx, num_segments=n_par * PB)
        summed = jnp.transpose(summed, (1, 0, 2)).reshape(K, n_par * PB * BLK)
        return total + summed, None

    start = jnp.zeros((K, n_par * PB * BLK), jnp.float32)
    result, _ = lax.scan(one_group, start, (jac_blocks, block_param, block_obs, block_count, obs_weight))
    return result
```

```python
import functools

import jax
import jax.numpy as jnp
from jax import lax
from jax.experimental import pallas as pl
from jax.experimental.pallas import tpu as pltpu
from jax.sharding import PartitionSpec as P

MESH = pl.DeviceIdType.MESH
STEP = 32
WIRE = jnp.float32


def fwd_kernel(bparam, bobs, count, omega_ref, blocks_ref, out_ref, acc):
    i = pl.program_id(0)
    oblocks = out_ref.shape[0]
    width = blocks_ref.shape[2]

    @pl.when(i == 0)
    def _():
        acc[...] = jnp.zeros_like(acc)

    for j in range(blocks_ref.shape[0]):
        s = i * blocks_ref.shape[0] + j
        to = jnp.where(s < count[0, 0], bobs[0, s], oblocks)
        at = pl.multiple_of(bparam[0, s] * width, width)
        acc[to] += jnp.dot(
            omega_ref[:, pl.ds(at, width)], blocks_ref[j], preferred_element_type=jnp.float32
        )

    @pl.when(i == pl.num_programs(0) - 1)
    def _():
        out_ref[...] = acc[0:oblocks]


def back_kernel(bparam, bobs, count, scaled_ref, blocks_ref, out_ref, acc):
    i = pl.program_id(0)
    pblocks = out_ref.shape[0]

    @pl.when(i == 0)
    def _():
        acc[...] = jnp.zeros_like(acc)

    for j in range(blocks_ref.shape[0]):
        s = i * blocks_ref.shape[0] + j
        to = jnp.where(s < count[0, 0], bparam[0, s], pblocks)
        acc[to] += lax.dot_general(
            scaled_ref[bobs[0, s]],
            blocks_ref[j],
            (((1,), (1,)), ((), ())),
            preferred_element_type=jnp.float32,
        )

    @pl.when(i == pl.num_programs(0) - 1)
    def _():
        out_ref[...] = acc[0:pblocks]


def sparse_call(kernel, bparam, bobs, count, dense, blocks, outs, probes):
    slots, width = blocks.shape[1], blocks.shape[2]
    whole = tuple(0 for _ in dense.shape)
    return pl.pallas_call(
        kernel,
        out_shape=jax.ShapeDtypeStruct((outs, probes, width), jnp.float32),
        grid_spec=pltpu.PrefetchScalarGridSpec(
            num_scalar_prefetch=3,
            grid=(slots // STEP,),
            in_specs=[
                pl.BlockSpec(dense.shape, lambda i, *_: whole),
                pl.BlockSpec((None, STEP, width, width), lambda i, *_: (0, i, 0, 0)),
            ],
            out_specs=pl.BlockSpec((outs, probes, width), lambda i, *_: (0, 0, 0)),
            scratch_shapes=[pltpu.VMEM((outs + 1, probes, width), jnp.float32)],
        ),
        compiler_params=pltpu.CompilerParams(vmem_limit_bytes=32 * 1024 * 1024),
        cost_estimate=pl.CostEstimate(
            flops=2 * slots * probes * width * width,
            bytes_accessed=2 * slots * width * width,
            transcendentals=0,
        ),
    )(bparam, bobs, count, dense, blocks)


def reduce_kernel(
    n, part_ref, weight_ref, out_ref, sib, sbuf, rbuf,
    s1, r1, s2, r2, s3, r3, s4, r4,
):
    me = lax.axis_index("par")
    chips = n // 2
    q, c = me // 2, lax.rem(me, 2)
    oblocks, _, width = part_ref.shape
    half = oblocks // 2
    nb = half // chips
    mate = {"par": 2 * q + 1 - c}

    def chip(i):
        return lax.rem(q + i, chips)

    def peer(t):
        return {"par": 2 * t + c}

    def mine(t):
        return pl.ds(c * half + t * nb, nb)

    def theirs(t):
        return pl.ds((1 - c) * half + t * nb, nb)

    barrier = pltpu.get_barrier_semaphore()
    pl.semaphore_signal(barrier, inc=1, device_id=mate, device_id_type=MESH)
    for i in range(1, chips):
        pl.semaphore_signal(barrier, inc=1, device_id=peer(chip(i)), device_id_type=MESH)
    pl.semaphore_wait(barrier, chips)

    def to_mate(t):
        return pltpu.make_async_remote_copy(
            src_ref=part_ref.at[theirs(t)], dst_ref=sib.at[t],
            send_sem=s1.at[t], recv_sem=r1.at[t], device_id=mate, device_id_type=MESH)

    def to_owner(t):
        return pltpu.make_async_remote_copy(
            src_ref=sbuf.at[t], dst_ref=rbuf.at[q],
            send_sem=s2.at[t], recv_sem=r2.at[q], device_id=peer(t), device_id_type=MESH)

    def from_chip(t):
        return pltpu.make_async_remote_copy(
            src_ref=sbuf.at[t], dst_ref=rbuf.at[t],
            send_sem=s2.at[t], recv_sem=r2.at[t], device_id=peer(t), device_id_type=MESH)

    def gather_to(t):
        return pltpu.make_async_remote_copy(
            src_ref=out_ref.at[mine(q)], dst_ref=out_ref.at[mine(q)],
            send_sem=s3.at[t], recv_sem=r3.at[q], device_id=peer(t), device_id_type=MESH)

    def gather_from(t):
        return pltpu.make_async_remote_copy(
            src_ref=out_ref.at[mine(t)], dst_ref=out_ref.at[mine(t)],
            send_sem=s3.at[t], recv_sem=r3.at[t], device_id=peer(t), device_id_type=MESH)

    def hand_over(t):
        return pltpu.make_async_remote_copy(
            src_ref=out_ref.at[mine(t)], dst_ref=out_ref.at[mine(t)],
            send_sem=s4.at[t], recv_sem=r4.at[t], device_id=mate, device_id_type=MESH)

    def take_over(t):
        return pltpu.make_async_remote_copy(
            src_ref=out_ref.at[theirs(t)], dst_ref=out_ref.at[theirs(t)],
            send_sem=s4.at[t], recv_sem=r4.at[t], device_id=mate, device_id_type=MESH)

    for i in range(1, chips + 1):
        to_mate(chip(i)).start()
    for i in range(1, chips):
        t = chip(i)
        to_mate(t).wait_recv()
        sbuf[t] = (part_ref[mine(t)] + sib[t]).astype(sbuf.dtype)
        to_owner(t).start()
    to_mate(q).wait_recv()
    total = part_ref[mine(q)] + sib[q]
    for i in range(1, chips):
        t = chip(chips - i)
        from_chip(t).wait_recv()
        total += rbuf[t].astype(jnp.float32)
    for b in range(nb):
        block = c * half + q * nb + b
        weight = weight_ref[0:1, pl.ds(pl.multiple_of(block * width, width), width)]
        out_ref[block] = (total[b] * weight).astype(out_ref.dtype)
    for i in range(1, chips):
        gather_to(chip(i)).start()
    hand_over(q).start()
    for i in range(1, chips):
        t = chip(chips - i)
        gather_from(t).wait_recv()
        hand_over(t).start()
    for i in range(chips):
        take_over(chip(i)).wait_recv()
    for i in range(chips):
        t = chip(i)
        to_mate(t).wait_send()
        hand_over(t).wait_send()
    for i in range(1, chips):
        t = chip(i)
        to_owner(t).wait_send()
        gather_to(t).wait_send()


def reduce_call(n, part, weights):
    oblocks, probes, width = part.shape
    chips = n // 2
    nb = oblocks // n
    dma = pltpu.SemaphoreType.DMA((chips,))
    vmem = pl.BlockSpec(memory_space=pltpu.VMEM)
    return pl.pallas_call(
        functools.partial(reduce_kernel, n),
        out_shape=jax.ShapeDtypeStruct(part.shape, jnp.bfloat16),
        in_specs=[vmem, vmem],
        out_specs=vmem,
        scratch_shapes=[
            pltpu.VMEM((chips, nb, probes, width), jnp.float32),
            pltpu.VMEM((chips, nb, probes, width), WIRE),
            pltpu.VMEM((chips, nb, probes, width), WIRE),
        ] + [dma] * 8,
        compiler_params=pltpu.CompilerParams(
            collective_id=0, has_side_effects=True, vmem_limit_bytes=32 * 1024 * 1024),
        cost_estimate=pl.CostEstimate(flops=0, bytes_accessed=4 * part.size, transcendentals=0),
    )(part, weights)


def exchange_kernel(groups, chunks, back_ref, out_ref, sbuf, rbuf, ss, rs):
    g = lax.axis_index("grp")
    pblocks, probes, width = back_ref.shape
    per = pblocks // groups
    cb = per // chunks

    def other(i):
        return lax.rem(g + i, groups)

    def copy(t, lands, k):
        return pltpu.make_async_remote_copy(
            src_ref=sbuf.at[t, pl.ds(k * cb, cb)], dst_ref=rbuf.at[lands, pl.ds(k * cb, cb)],
            send_sem=ss.at[t, k], recv_sem=rs.at[lands, k],
            device_id={"grp": t}, device_id_type=MESH)

    barrier = pltpu.get_barrier_semaphore()
    for i in range(1, groups):
        pl.semaphore_signal(barrier, inc=1, device_id={"grp": other(i)}, device_id_type=MESH)
    pl.semaphore_wait(barrier, groups - 1)

    for k in range(chunks):
        for i in range(1, groups):
            t = other(i)
            sbuf[t, k * cb:(k + 1) * cb] = back_ref[pl.ds(t * per + k * cb, cb)].astype(sbuf.dtype)
            copy(t, g, k).start()
    for k in range(chunks):
        for i in range(1, groups):
            copy(other(i), other(i), k).wait_recv()
        for b in range(k * cb, (k + 1) * cb):
            total = back_ref[g * per + b]
            for i in range(1, groups):
                total += rbuf[other(i), b].astype(jnp.float32)
            out_ref[:, b * width:(b + 1) * width] = total
    for k in range(chunks):
        for i in range(1, groups):
            copy(other(i), g, k).wait_send()


def exchange_call(groups, back):
    pblocks, probes, width = back.shape
    per = pblocks // groups
    chunks = min(4, per)
    vmem = pl.BlockSpec(memory_space=pltpu.VMEM)
    return pl.pallas_call(
        functools.partial(exchange_kernel, groups, chunks),
        out_shape=jax.ShapeDtypeStruct((probes, per * width), jnp.float32),
        in_specs=[vmem],
        out_specs=vmem,
        scratch_shapes=[
            pltpu.VMEM((groups, per, probes, width), jnp.bfloat16),
            pltpu.VMEM((groups, per, probes, width), jnp.bfloat16),
            pltpu.SemaphoreType.DMA((groups, chunks)),
            pltpu.SemaphoreType.DMA((groups, chunks)),
        ],
        compiler_params=pltpu.CompilerParams(
            collective_id=1, has_side_effects=True, vmem_limit_bytes=32 * 1024 * 1024),
        cost_estimate=pl.CostEstimate(flops=0, bytes_accessed=4 * back.size, transcendentals=0),
    )(back)


def on_device(groups, n, omega, blocks, bparam, bobs, count, weights):
    probes = omega.shape[0]
    width = blocks.shape[2]
    oblocks = weights.shape[1] // width
    pblocks = omega.shape[1] // width
    part = sparse_call(fwd_kernel, bparam, bobs, count, omega, blocks, oblocks, probes)
    scaled = reduce_call(n, part, weights)
    back = sparse_call(back_kernel, bparam, bobs, count, scaled, blocks, pblocks, probes)
    return exchange_call(groups, back)


def solution(mesh):
    in_specs = (
        P(None, "par"),
        P("grp", "par", None, None),
        P("grp", "par"),
        P("grp", "par"),
        P("grp", "par"),
        P("grp", None),
    )
    out_specs = P(None, ("par", "grp"))
    body = functools.partial(on_device, mesh.shape["grp"], mesh.shape["par"])
    return jax.shard_map(
        body, mesh=mesh, in_specs=in_specs, out_specs=out_specs, check_vma=False
    )
```

```python
import functools

import jax
import jax.numpy as jnp
from jax import lax
from jax.experimental import pallas as pl
from jax.experimental.pallas import tpu as pltpu
from jax.sharding import PartitionSpec as P

MESH = pl.DeviceIdType.MESH
STEP = 32
LEVELS = 32000.0
VMEM_LIMIT = 16 * 1024 * 1024


def fwd_kernel(bparam, bobs, count, omega, blocks, acc):
    oblocks = acc.shape[0] - 1
    slots, width = blocks.shape[1], blocks.shape[2]
    acc[...] = jnp.zeros_like(acc)

    def step(i, carry):
        for j in range(STEP):
            s = i * STEP + j
            to = jnp.where(s < count[0, 0], bobs[0, s], oblocks)
            at = pl.multiple_of(bparam[0, s] * width, width)
            acc[to] += jnp.dot(
                omega[:, pl.ds(at, width)], blocks[0, s], preferred_element_type=jnp.float32
            )
        return carry

    lax.fori_loop(0, slots // STEP, step, 0)


def fwd_call(bparam, bobs, count, omega, blocks, oblocks):
    probes = omega.shape[0]
    slots, width = blocks.shape[1], blocks.shape[2]
    smem = pl.BlockSpec(memory_space=pltpu.SMEM)
    vmem = pl.BlockSpec(memory_space=pltpu.VMEM)
    return pl.pallas_call(
        fwd_kernel,
        out_shape=jax.ShapeDtypeStruct((oblocks + 1, probes, width), jnp.float32),
        in_specs=[smem, smem, smem, vmem, vmem],
        out_specs=vmem,
        compiler_params=pltpu.CompilerParams(vmem_limit_bytes=VMEM_LIMIT),
        cost_estimate=pl.CostEstimate(
            flops=2 * slots * probes * width * width,
            bytes_accessed=2 * slots * width * width, transcendentals=0),
    )(bparam, bobs, count, omega, blocks)


def back_kernel(bparam, bobs, count, scaled_ref, blocks_ref, acc):
    pblocks = acc.shape[0] - 1
    slots = blocks_ref.shape[1]
    acc[...] = jnp.zeros_like(acc)

    def step(i, carry):
        for j in range(STEP):
            s = i * STEP + j
            to = jnp.where(s < count[0, 0], bparam[0, s], pblocks)
            acc[to] += lax.dot_general(
                scaled_ref[bobs[0, s]], blocks_ref[0, s],
                (((1,), (1,)), ((), ())), preferred_element_type=jnp.float32)
        return carry

    lax.fori_loop(0, slots // (STEP), step, 0)


def back_call(bparam, bobs, count, scaled, blocks, pblocks):
    probes = scaled.shape[1]
    slots, width = blocks.shape[1], blocks.shape[2]
    smem = pl.BlockSpec(memory_space=pltpu.SMEM)
    vmem = pl.BlockSpec(memory_space=pltpu.VMEM)
    return pl.pallas_call(
        back_kernel,
        out_shape=jax.ShapeDtypeStruct((pblocks + 1, probes, width), jnp.float32),
        in_specs=[smem, smem, smem, vmem, vmem],
        out_specs=vmem,
        compiler_params=pltpu.CompilerParams(vmem_limit_bytes=VMEM_LIMIT),
        cost_estimate=pl.CostEstimate(
            flops=2 * slots * probes * width * width,
            bytes_accessed=2 * slots * width * width, transcendentals=0),
    )(bparam, bobs, count, scaled, blocks)


def reduce_kernel(
    n, part_ref, weight_ref, out_ref, sib, sbuf, rbuf, sscale, rscale,
    s1, r1, s2, r2, s3, r3, s4, r4, s5, r5, s6,
):
    me = lax.axis_index("par")
    chips = n // 2
    rows = 2
    cols = chips // rows
    q, c = me // 2, lax.rem(me, 2)
    z, y = q // rows, lax.rem(q, rows)
    oblocks, width = out_ref.shape[0], out_ref.shape[2]
    half = oblocks // 2
    nb = half // chips
    mate = {"par": 2 * q + 1 - c}
    beside = rows * z + 1 - y

    def chip(i):
        return lax.rem(q + i, chips)

    def in_row(i):
        return rows * lax.rem(z + i, cols) + y

    def in_other_row(i):
        return rows * lax.rem(z + i, cols) + 1 - y

    def peer(t):
        return {"par": 2 * t + c}

    def mine(t):
        return pl.ds(c * half + t * nb, nb)

    def theirs(t):
        return pl.ds((1 - c) * half + t * nb, nb)

    barrier = pltpu.get_barrier_semaphore()
    pl.semaphore_signal(barrier, inc=1, device_id=mate, device_id_type=MESH)
    for i in range(1, chips):
        pl.semaphore_signal(barrier, inc=1, device_id=peer(chip(i)), device_id_type=MESH)
    pl.semaphore_wait(barrier, chips)

    def remote(src, dst, send, recv, device):
        return pltpu.make_async_remote_copy(
            src_ref=src, dst_ref=dst, send_sem=send, recv_sem=recv,
            device_id=device, device_id_type=MESH)

    def to_mate(t):
        return remote(part_ref.at[theirs(t)], sib.at[t], s1.at[t], r1.at[t], mate)

    def to_owner(t, lands):
        return remote(sbuf.at[t], rbuf.at[lands], s2.at[t], r2.at[lands], peer(t))

    def scale_to_owner(t, lands):
        return remote(sscale.at[t], rscale.at[lands], s5.at[t], r5.at[lands], peer(t))

    def gather(piece, to, sems, at):
        return remote(
            out_ref.at[mine(piece)], out_ref.at[mine(piece)], sems.at[at], r3.at[piece], peer(to))

    def hand_over(t):
        return remote(out_ref.at[mine(t)], out_ref.at[mine(t)], s4.at[t], r4.at[t], mate)

    def take_over(t):
        return remote(out_ref.at[theirs(t)], out_ref.at[theirs(t)], s4.at[t], r4.at[t], mate)

    for i in range(1, chips + 1):
        to_mate(chip(i)).start()
    for i in range(1, chips):
        t = chip(i)
        to_mate(t).wait_recv()
        value = part_ref[mine(t)] + sib[t]
        largest = jnp.max(jnp.max(jnp.abs(value), axis=0), axis=0, keepdims=True)
        largest = jnp.maximum(largest, 1e-30)
        sscale[t] = jnp.broadcast_to(largest * (1.0 / LEVELS), sscale.shape[1:])
        scale_to_owner(t, q).start()
        level = jnp.round(value * (LEVELS / largest)[None])
        sbuf[t] = level.astype(jnp.int32).astype(sbuf.dtype)
        to_owner(t, q).start()
    to_mate(q).wait_recv()
    total = part_ref[mine(q)] + sib[q]
    for i in range(1, chips):
        t = chip(chips - i)
        scale_to_owner(t, t).wait_recv()
        to_owner(t, t).wait_recv()
        level = rbuf[t].astype(jnp.int32).astype(jnp.float32)
        total += level * rscale[t][0:1][None]
    for b in range(nb):
        block = c * half + q * nb + b
        weight = weight_ref[0:1, pl.ds(pl.multiple_of(block * width, width), width)]
        out_ref[block] = (total[b] * weight).astype(out_ref.dtype)

    gather(q, beside, s6, q).start()
    for i in range(1, cols):
        gather(q, in_row(i), s3, in_row(i)).start()
    hand_over(q).start()
    for i in range(1, cols):
        t = in_row(cols - i)
        gather(t, t, s3, t).wait_recv()
        gather(t, beside, s6, t).start()
        hand_over(t).start()
    for i in range(cols):
        t = in_other_row((cols - i) % cols)
        gather(t, t, s3, t).wait_recv()
        hand_over(t).start()
    for i in range(chips):
        take_over(chip(i)).wait_recv()
    for i in range(chips):
        t = chip(i)
        to_mate(t).wait_send()
        hand_over(t).wait_send()
    for i in range(1, chips):
        t = chip(i)
        to_owner(t, q).wait_send()
        scale_to_owner(t, q).wait_send()
    for i in range(cols):
        gather(in_row(i), beside, s6, in_row(i)).wait_send()
    for i in range(1, cols):
        gather(q, in_row(i), s3, in_row(i)).wait_send()


def reduce_call(n, part, weights):
    oblocks, probes, width = part.shape[0] - 1, part.shape[1], part.shape[2]
    chips = n // 2
    nb = oblocks // n
    dma = pltpu.SemaphoreType.DMA((chips,))
    vmem = pl.BlockSpec(memory_space=pltpu.VMEM)
    return pl.pallas_call(
        functools.partial(reduce_kernel, n),
        out_shape=jax.ShapeDtypeStruct((oblocks, probes, width), jnp.bfloat16),
        in_specs=[vmem, vmem],
        out_specs=vmem,
        scratch_shapes=[
            pltpu.VMEM((chips, nb, probes, width), jnp.float32),
            pltpu.VMEM((chips, nb, probes, width), jnp.int16),
            pltpu.VMEM((chips, nb, probes, width), jnp.int16),
            pltpu.VMEM((chips, 8, width), jnp.float32),
            pltpu.VMEM((chips, 8, width), jnp.float32),
        ] + [dma] * 11,
        compiler_params=pltpu.CompilerParams(
            collective_id=0, has_side_effects=True, vmem_limit_bytes=VMEM_LIMIT),
        cost_estimate=pl.CostEstimate(flops=0, bytes_accessed=4 * part.size, transcendentals=0),
    )(part, weights)


def exchange_kernel(groups, chunks, back_ref, out_ref, sbuf, rbuf, ss, rs):
    g = lax.axis_index("grp")
    pblocks, width = back_ref.shape[0] - 1, back_ref.shape[2]
    per = pblocks // groups
    cb = per // chunks

    def other(i):
        return lax.rem(g + i, groups)

    def copy(t, lands, k):
        return pltpu.make_async_remote_copy(
            src_ref=sbuf.at[t, pl.ds(k * cb, cb)], dst_ref=rbuf.at[lands, pl.ds(k * cb, cb)],
            send_sem=ss.at[t, k], recv_sem=rs.at[lands, k],
            device_id={"grp": t}, device_id_type=MESH)

    barrier = pltpu.get_barrier_semaphore()
    for i in range(1, groups):
        pl.semaphore_signal(barrier, inc=1, device_id={"grp": other(i)}, device_id_type=MESH)
    pl.semaphore_wait(barrier, groups - 1)

    for k in range(chunks):
        for i in range(1, groups):
            t = other(i)
            sbuf[t, k * cb:(k + 1) * cb] = back_ref[pl.ds(t * per + k * cb, cb)].astype(sbuf.dtype)
            copy(t, g, k).start()
    for k in range(chunks):
        for i in range(1, groups):
            copy(other(i), other(i), k).wait_recv()
        for b in range(k * cb, (k + 1) * cb):
            total = back_ref[g * per + b]
            for i in range(1, groups):
                total += rbuf[other(i), b].astype(jnp.float32)
            out_ref[:, b * width:(b + 1) * width] = total
    for k in range(chunks):
        for i in range(1, groups):
            copy(other(i), g, k).wait_send()


def exchange_call(groups, back):
    pblocks, probes, width = back.shape[0] - 1, back.shape[1], back.shape[2]
    per = pblocks // groups
    chunks = min(4, per)
    vmem = pl.BlockSpec(memory_space=pltpu.VMEM)
    return pl.pallas_call(
        functools.partial(exchange_kernel, groups, chunks),
        out_shape=jax.ShapeDtypeStruct((probes, per * width), jnp.float32),
        in_specs=[vmem],
        out_specs=vmem,
        scratch_shapes=[
            pltpu.VMEM((groups, per, probes, width), jnp.bfloat16),
            pltpu.VMEM((groups, per, probes, width), jnp.bfloat16),
            pltpu.SemaphoreType.DMA((groups, chunks)),
            pltpu.SemaphoreType.DMA((groups, chunks)),
        ],
        compiler_params=pltpu.CompilerParams(
            collective_id=1, has_side_effects=True, vmem_limit_bytes=VMEM_LIMIT),
        cost_estimate=pl.CostEstimate(flops=0, bytes_accessed=4 * back.size, transcendentals=0),
    )(back)


def on_device(groups, n, omega, blocks, bparam, bobs, count, weights):
    width = blocks.shape[2]
    oblocks = weights.shape[1] // width
    pblocks = omega.shape[1] // width
    part = fwd_call(bparam, bobs, count, omega, blocks, oblocks)
    scaled = reduce_call(n, part, weights)
    back = back_call(bparam, bobs, count, scaled, blocks, pblocks)
    return exchange_call(groups, back)


def solution(mesh):
    in_specs = (
        P(None, "par"),
        P("grp", "par", None, None),
        P("grp", "par"),
        P("grp", "par"),
        P("grp", "par"),
        P("grp", None),
    )
    out_specs = P(None, ("par", "grp"))
    body = functools.partial(on_device, mesh.shape["grp"], mesh.shape["par"])
    return jax.shard_map(
        body, mesh=mesh, in_specs=in_specs, out_specs=out_specs, check_vma=False
    )
```

```python
import functools

import jax
import jax.numpy as jnp
from jax import lax
from jax.experimental import pallas as pl
from jax.experimental.pallas import tpu as pltpu
from jax.sharding import PartitionSpec as P

MESH = pl.DeviceIdType.MESH
STEP = 16
ROWS = 16
LEVELS = 32000.0
VMEM_LIMIT = 57 * 1024 * 1024


def kernel(
    n, groups,
    bparam_hbm, bobs_hbm, count, omega_hbm, blocks_hbm, weight_hbm, out_ref,
    bparam, bobs, bparam_row, bobs_row, omega, panels, weight, blocks,
    terms, part, scaled, sib, sbuf, rbuf, sscale, rscale, own, half_out, xsend, xrecv,
    small, big, s1, r1, s2, r2, s3, r3, s4, r4, s5, r5, s6, sx, rx,
):
    me = lax.axis_index("par")
    g = lax.axis_index("grp")
    probes = omega.shape[0]
    slots, width = blocks.shape[0], blocks.shape[1]
    oblocks = weight.shape[1] // width
    pblocks = omega.shape[1] // width
    per = pblocks // groups
    chips = n // 2
    rows = 2
    cols = chips // rows
    q, c = me // 2, lax.rem(me, 2)
    z, y = q // rows, lax.rem(q, rows)
    half = oblocks // 2
    nb = half // chips
    mate = {"par": 2 * q + 1 - c}
    beside = rows * z + 1 - y

    def chip(i):
        return lax.rem(q + i, chips)

    def in_row(i):
        return rows * lax.rem(z + i, cols) + y

    def in_other_row(i):
        return rows * lax.rem(z + i, cols) + 1 - y

    def peer(t):
        return {"par": 2 * t + c}

    def other(i):
        return lax.rem(g + i, groups)

    def lines(block, count_of):
        return pl.ds(pl.multiple_of(block * probes, probes), count_of * probes)

    def mine(t):
        return pl.ds(c * half + t * nb, nb)

    def theirs(t):
        return pl.ds((1 - c) * half + t * nb, nb)

    early = [
        pltpu.make_async_copy(bparam_hbm, bparam, small.at[0]),
        pltpu.make_async_copy(bobs_hbm, bobs, small.at[1]),
        pltpu.make_async_copy(omega_hbm, omega, small.at[2]),
        pltpu.make_async_copy(bparam_hbm, bparam_row, small.at[3]),
        pltpu.make_async_copy(bobs_hbm, bobs_row, small.at[4]),
        pltpu.make_async_copy(weight_hbm, weight, small.at[5]),
    ]

    def blocks_of(i):
        at = pl.ds(i * STEP, STEP)
        return pltpu.make_async_copy(blocks_hbm.at[0, at], blocks.at[at], big.at[i])

    for copy in early:
        copy.start()
    for i in range(slots // STEP):
        blocks_of(i).start()

    barrier = pltpu.get_barrier_semaphore()
    pl.semaphore_signal(barrier, inc=1, device_id=mate, device_id_type=MESH)
    for i in range(1, chips):
        pl.semaphore_signal(barrier, inc=1, device_id=peer(chip(i)), device_id_type=MESH)
    for i in range(1, groups):
        pl.semaphore_signal(barrier, inc=1, device_id={"grp": other(i)}, device_id_type=MESH)

    for copy in early:
        copy.wait()
    for b in range(pblocks):
        panels[b] = omega[:, b * width:(b + 1) * width]

    def fwd_step(i, carry):
        blocks_of(i).wait()
        for j in range(STEP):
            s = i * STEP + j
            terms[lines(s, 1)] = jnp.dot(
                panels[bparam[0, s]], blocks[s], preferred_element_type=jnp.float32)
        return carry

    lax.fori_loop(0, slots // STEP, fwd_step, 0)

    used = lax.broadcasted_iota(jnp.int32, (1, slots), 1) < count[0, 0]

    def chooser(row, first, length):
        place = lax.broadcasted_iota(jnp.int32, (length, slots), 0) + first
        chosen = jnp.where((place == row) & used, 1.0, 0.0).astype(jnp.bfloat16)
        return jnp.concatenate([chosen, chosen], axis=1)

    def summed(chosen, k):
        value = terms[pl.ds(k, slots, stride=probes), :]
        high = value.astype(jnp.bfloat16)
        low = (value - high.astype(jnp.float32)).astype(jnp.bfloat16)
        return jnp.dot(
            chosen, jnp.concatenate([high, low], axis=0), preferred_element_type=jnp.float32)

    by_obs = chooser(bobs_row[...], 0, oblocks)
    for k in range(probes):
        part[pl.ds(k, oblocks, stride=probes), :] = summed(by_obs, k)

    def remote(src, dst, send, recv, device):
        return pltpu.make_async_remote_copy(
            src_ref=src, dst_ref=dst, send_sem=send, recv_sem=recv,
            device_id=device, device_id_type=MESH)

    def to_mate(t):
        return remote(
            part.at[lines((1 - c) * half + t * nb, nb)], sib.at[t], s1.at[t], r1.at[t], mate)

    def to_owner(t, lands):
        return remote(sbuf.at[t], rbuf.at[lands], s2.at[t], r2.at[lands], peer(t))

    def scale_to_owner(t, lands):
        return remote(sscale.at[t], rscale.at[lands], s5.at[t], r5.at[lands], peer(t))

    def gather(piece, to, sems, at):
        return remote(
            scaled.at[mine(piece)], scaled.at[mine(piece)], sems.at[at], r3.at[piece], peer(to))

    def hand_over(t):
        return remote(scaled.at[mine(t)], scaled.at[mine(t)], s4.at[t], r4.at[t], mate)

    def take_over(t):
        return remote(scaled.at[theirs(t)], scaled.at[theirs(t)], s4.at[t], r4.at[t], mate)

    pl.semaphore_wait(barrier, chips + groups - 1)
    for i in range(1, chips + 1):
        to_mate(chip(i)).start()
    for i in range(1, chips):
        t = chip(i)
        to_mate(t).wait_recv()
        value = part[lines(c * half + t * nb, nb), :] + sib[t]
        largest = jnp.max(jnp.abs(value), axis=0, keepdims=True)
        largest = jnp.maximum(largest, 1e-30)
        sscale[t] = jnp.broadcast_to(largest * (1.0 / LEVELS), sscale.shape[1:])
        scale_to_owner(t, q).start()
        level = jnp.round(value * (LEVELS / largest))
        sbuf[t] = level.astype(jnp.int32).astype(sbuf.dtype)
        to_owner(t, q).start()
    to_mate(q).wait_recv()
    total = part[lines(c * half + q * nb, nb), :] + sib[q]
    for i in range(1, chips):
        t = chip(chips - i)
        scale_to_owner(t, t).wait_recv()
        to_owner(t, t).wait_recv()
        total += rbuf[t].astype(jnp.int32).astype(jnp.float32) * rscale[t][0:1]
    for b in range(nb):
        block = c * half + q * nb + b
        factor = weight[0:1, pl.ds(pl.multiple_of(block * width, width), width)]
        scaled[block] = (total[b * probes:(b + 1) * probes] * factor).astype(scaled.dtype)

    gather(q, beside, s6, q).start()
    for i in range(1, cols):
        gather(q, in_row(i), s3, in_row(i)).start()
    hand_over(q).start()
    for i in range(1, cols):
        t = in_row(cols - i)
        gather(t, t, s3, t).wait_recv()
        gather(t, beside, s6, t).start()
        hand_over(t).start()
    for i in range(cols):
        t = in_other_row((cols - i) % cols)
        gather(t, t, s3, t).wait_recv()
        hand_over(t).start()
    for i in range(chips):
        take_over(chip(i)).wait_recv()

    def back_step(i, carry):
        for j in range(STEP):
            s = i * STEP + j
            terms[lines(s, 1)] = lax.dot_general(
                scaled[bobs[0, s]], blocks[s],
                (((1,), (1,)), ((), ())), preferred_element_type=jnp.float32)
        return carry

    lax.fori_loop(0, slots // STEP, back_step, 0)

    def exchange(t, lands, h):
        return remote(
            xsend.at[t, h], xrecv.at[lands, h], sx.at[t, h], rx.at[lands, h], {"grp": t})

    parts = probes // ROWS
    for i in range(1, groups):
        t = other(i)
        chosen = chooser(bparam_row[...], t * per, per)
        for h in range(parts):
            for k in range(ROWS):
                half_out[pl.ds(k, per, stride=ROWS), :] = summed(chosen, h * ROWS + k)
            xsend[t, h] = half_out[...].astype(xsend.dtype)
            exchange(t, g, h).start()
    chosen = chooser(bparam_row[...], g * per, per)
    for k in range(probes):
        own[pl.ds(k, per, stride=probes), :] = summed(chosen, k)
    for h in range(parts):
        for i in range(1, groups):
            exchange(other(i), other(i), h).wait_recv()
        for b in range(per):
            value = own[b * probes + h * ROWS:b * probes + (h + 1) * ROWS, :]
            for i in range(1, groups):
                value += xrecv[other(i), h, b * ROWS:(b + 1) * ROWS, :].astype(jnp.float32)
            out_ref[h * ROWS:(h + 1) * ROWS, b * width:(b + 1) * width] = value

    for i in range(chips):
        t = chip(i)
        to_mate(t).wait_send()
        hand_over(t).wait_send()
    for i in range(1, chips):
        t = chip(i)
        to_owner(t, q).wait_send()
        scale_to_owner(t, q).wait_send()
    for i in range(cols):
        gather(in_row(i), beside, s6, in_row(i)).wait_send()
    for i in range(1, cols):
        gather(q, in_row(i), s3, in_row(i)).wait_send()
    for i in range(1, groups):
        for h in range(parts):
            exchange(other(i), g, h).wait_send()


def on_device(groups, n, omega, blocks, bparam, bobs, count, weights):
    probes = omega.shape[0]
    slots, width = blocks.shape[1], blocks.shape[2]
    oblocks = weights.shape[1] // width
    pblocks = omega.shape[1] // width
    per = pblocks // groups
    chips = n // 2
    piece = oblocks // n * probes
    parts = probes // ROWS
    dma = pltpu.SemaphoreType.DMA
    hbm = pl.BlockSpec(memory_space=pl.ANY)
    return pl.pallas_call(
        functools.partial(kernel, n, groups),
        out_shape=jax.ShapeDtypeStruct((probes, per * width), jnp.float32),
        in_specs=[hbm, hbm, pl.BlockSpec(memory_space=pltpu.SMEM), hbm, hbm, hbm],
        out_specs=pl.BlockSpec(memory_space=pltpu.VMEM),
        scratch_shapes=[
            pltpu.SMEM(bparam.shape, jnp.int32),
            pltpu.SMEM(bobs.shape, jnp.int32),
            pltpu.VMEM(bparam.shape, jnp.int32),
            pltpu.VMEM(bobs.shape, jnp.int32),
            pltpu.VMEM(omega.shape, omega.dtype),
            pltpu.VMEM((pblocks, probes, width), omega.dtype),
            pltpu.VMEM(weights.shape, weights.dtype),
            pltpu.VMEM(blocks.shape[1:], blocks.dtype),
            pltpu.VMEM((slots * probes, width), jnp.float32),
            pltpu.VMEM((oblocks * probes, width), jnp.float32),
            pltpu.VMEM((oblocks, probes, width), jnp.bfloat16),
            pltpu.VMEM((chips, piece, width), jnp.float32),
            pltpu.VMEM((chips, piece, width), jnp.int16),
            pltpu.VMEM((chips, piece, width), jnp.int16),
            pltpu.VMEM((chips, 8, width), jnp.float32),
            pltpu.VMEM((chips, 8, width), jnp.float32),
            pltpu.VMEM((per * probes, width), jnp.float32),
            pltpu.VMEM((per * ROWS, width), jnp.float32),
            pltpu.VMEM((groups, parts, per * ROWS, width), jnp.bfloat16),
            pltpu.VMEM((groups, parts, per * ROWS, width), jnp.bfloat16),
            dma((6,)),
            dma((slots // STEP,)),
        ] + [dma((chips,))] * 11 + [dma((groups, parts))] * 2,
        compiler_params=pltpu.CompilerParams(
            collective_id=0, has_side_effects=True, vmem_limit_bytes=VMEM_LIMIT),
        cost_estimate=pl.CostEstimate(
            flops=4 * slots * probes * width * width,
            bytes_accessed=2 * slots * width * width, transcendentals=0),
    )(bparam, bobs, count, omega, blocks, weights)


def solution(mesh):
    in_specs = (
        P(None, "par"),
        P("grp", "par", None, None),
        P("grp", "par"),
        P("grp", "par"),
        P("grp", "par"),
        P("grp", None),
    )
    out_specs = P(None, ("par", "grp"))
    body = functools.partial(on_device, mesh.shape["grp"], mesh.shape["par"])
    return jax.shard_map(
        body, mesh=mesh, in_specs=in_specs, out_specs=out_specs, check_vma=False
    )
```

```python
import functools

import jax
import jax.numpy as jnp
from jax import lax
from jax.experimental import pallas as pl
from jax.experimental.pallas import tpu as pltpu
from jax.sharding import PartitionSpec as P

MESH = pl.DeviceIdType.MESH
STEP = 16
ROWS = 16
LEVELS = 32000.0
VMEM_LIMIT = 57 * 1024 * 1024


def kernel(
    n, groups,
    bparam_hbm, bobs_hbm, count, omega_hbm, blocks_hbm, weight_hbm, own_ref, xrecv,
    bparam, bobs, bparam_row, bobs_row, omega, panels, weight, blocks,
    terms, part, scaled, sib, sbuf, rbuf, sscale, rscale, zsbuf, zrbuf, zsscale, zrscale,
    half_out, xsend,
    small, big, s1, r1, s2, r2, s3, r3, s4, r4, s5, r5, s6, s7, r7, s8, r8, sx, rx,
):
    me = lax.axis_index("par")
    g = lax.axis_index("grp")
    probes = omega.shape[0]
    slots, width = blocks.shape[0], blocks.shape[1]
    oblocks = weight.shape[1] // width
    pblocks = omega.shape[1] // width
    per = pblocks // groups
    chips = n // 2
    rows = 2
    cols = chips // rows
    q, c = me // 2, lax.rem(me, 2)
    z, y = q // rows, lax.rem(q, rows)
    half = oblocks // 2
    nb = half // chips
    mate = {"par": 2 * q + 1 - c}
    beside = {"par": 2 * (rows * z + 1 - y) + c}

    parts = probes // ROWS

    def zed(i):
        return lax.rem(z + i, cols)

    def at_z(i):
        return {"par": 2 * (rows * zed(i) + y) + c}

    def other(i):
        return lax.rem(g + i, groups)

    def lines(block, length):
        return pl.ds(pl.multiple_of(block * probes, probes), length * probes)

    def part_lines(h, block, length):
        at = (h * oblocks + block) * ROWS
        return pl.ds(pl.multiple_of(at, ROWS), length * ROWS)

    def mine(p):
        return pl.ds(c * half + p * nb, nb)

    def theirs(p):
        return pl.ds((1 - c) * half + p * nb, nb)

    early = [
        pltpu.make_async_copy(bparam_hbm, bparam, small.at[0]),
        pltpu.make_async_copy(bobs_hbm, bobs, small.at[1]),
        pltpu.make_async_copy(omega_hbm, omega, small.at[2]),
        pltpu.make_async_copy(bparam_hbm, bparam_row, small.at[3]),
        pltpu.make_async_copy(bobs_hbm, bobs_row, small.at[4]),
        pltpu.make_async_copy(weight_hbm, weight, small.at[5]),
    ]

    def blocks_of(i):
        at = pl.ds(i * STEP, STEP)
        return pltpu.make_async_copy(blocks_hbm.at[0, at], blocks.at[at], big.at[i])

    for copy in early:
        copy.start()
    for i in range(slots // STEP):
        blocks_of(i).start()

    barrier = pltpu.get_barrier_semaphore()
    pl.semaphore_signal(barrier, inc=1, device_id=mate, device_id_type=MESH)
    pl.semaphore_signal(barrier, inc=1, device_id=beside, device_id_type=MESH)
    for i in range(1, cols):
        pl.semaphore_signal(barrier, inc=1, device_id=at_z(i), device_id_type=MESH)
    for i in range(1, groups):
        pl.semaphore_signal(barrier, inc=1, device_id={"grp": other(i)}, device_id_type=MESH)

    for copy in early:
        copy.wait()
    for b in range(pblocks):
        panels[b] = omega[:, b * width:(b + 1) * width]

    def fwd_step(i, carry):
        blocks_of(i).wait()
        for j in range(STEP):
            s = i * STEP + j
            terms[lines(s, 1)] = jnp.dot(
                panels[bparam[0, s]], blocks[s], preferred_element_type=jnp.float32)
        return carry

    lax.fori_loop(0, slots // STEP, fwd_step, 0)

    used = lax.broadcasted_iota(jnp.int32, (1, slots), 1) < count[0, 0]

    def chooser(row, first, length):
        place = lax.broadcasted_iota(jnp.int32, (length, slots), 0) + first
        chosen = jnp.where((place == row) & used, 1.0, 0.0).astype(jnp.bfloat16)
        return jnp.concatenate([chosen, chosen], axis=1)

    def summed(chosen, k):
        value = terms[pl.ds(k, slots, stride=probes), :]
        high = value.astype(jnp.bfloat16)
        low = (value - high.astype(jnp.float32)).astype(jnp.bfloat16)
        return jnp.dot(
            chosen, jnp.concatenate([high, low], axis=0), preferred_element_type=jnp.float32)

    def remote(src, dst, send, recv, device):
        return pltpu.make_async_remote_copy(
            src_ref=src, dst_ref=dst, send_sem=send, recv_sem=recv,
            device_id=device, device_id_type=MESH)

    row_blocks = cols * nb

    def to_mate(h, r):
        return remote(
            part.at[part_lines(h, (1 - c) * half + r * row_blocks, row_blocks)],
            sib.at[h, r], s1.at[h, r], r1.at[h, r], mate)

    def to_beside(h):
        return remote(sbuf.at[h], rbuf.at[h], s2.at[h], r2.at[h], beside)

    def scale_to_beside(h):
        return remote(sscale.at[h], rscale.at[h], s5.at[h], r5.at[h], beside)

    def to_z(h, i, lands):
        return remote(
            zsbuf.at[h, zed(i)], zrbuf.at[h, lands], s7.at[h, zed(i)], r7.at[h, lands], at_z(i))

    def scale_to_z(h, i, lands):
        return remote(zsscale.at[h], zrscale.at[h, lands], s8.at[h, zed(i)], r8.at[h, lands], at_z(i))

    def gather_z(h, p, i):
        piece = scaled.at[h, mine(p)]
        return remote(piece, piece, s3.at[h, zed(i)], r3.at[h, p], at_z(i))

    def gather_beside(h, p):
        piece = scaled.at[h, mine(p)]
        return remote(piece, piece, s6.at[h, p], r3.at[h, p], beside)

    def hand_over(h, p):
        piece = scaled.at[h, mine(p)]
        return remote(piece, piece, s4.at[h, p], r4.at[h, p], mate)

    def take_over(h, p):
        piece = scaled.at[h, theirs(p)]
        return remote(piece, piece, s4.at[h, p], r4.at[h, p], mate)

    def coded(value):
        largest = jnp.maximum(jnp.max(jnp.abs(value), axis=0, keepdims=True), 1e-30)
        level = jnp.round(value * (LEVELS / largest)).astype(jnp.int32).astype(jnp.int16)
        return level, jnp.broadcast_to(largest * (1.0 / LEVELS), (8, width))

    def decoded(level, scale):
        return level.astype(jnp.int32).astype(jnp.float32) * scale[0:1]

    def row_sum(h, r):
        to_mate(h, r).wait_recv()
        return part[part_lines(h, c * half + r * row_blocks, row_blocks), :] + sib[h, r]

    by_obs = chooser(bobs_row[...], 0, oblocks)
    for h in range(parts):
        for k in range(ROWS):
            part[pl.ds(h * oblocks * ROWS + k, oblocks, stride=ROWS), :] = summed(
                by_obs, h * ROWS + k)
        if h == 0:
            pl.semaphore_wait(barrier, cols + groups)
        to_mate(h, 1 - y).start()
        to_mate(h, y).start()
    for h in range(parts):
        level, scale = coded(row_sum(h, 1 - y))
        sscale[h] = scale
        scale_to_beside(h).start()
        sbuf[h] = level
        to_beside(h).start()
    totals = []
    for h in range(parts):
        value = row_sum(h, y)
        scale_to_beside(h).wait_recv()
        to_beside(h).wait_recv()
        value += decoded(rbuf[h], rscale[h])
        level, scale = coded(value)
        zsscale[h] = scale
        piece = nb * ROWS
        for j in range(cols):
            zsbuf[h, j] = level[j * piece:(j + 1) * piece]
        sib[h, y] = value
        for i in range(1, cols):
            scale_to_z(h, i, z).start()
            to_z(h, i, z).start()
    for h in range(parts):
        at = pl.ds(pl.multiple_of(z * piece, piece), piece)
        total = sib[h, y, at, :]
        for i in range(1, cols):
            scale_to_z(h, i, zed(i)).wait_recv()
            to_z(h, i, zed(i)).wait_recv()
            total += decoded(zrbuf[h, zed(i)], zrscale[h, zed(i)])
        p = y * cols + z
        for b in range(nb):
            block = c * half + p * nb + b
            factor = weight[0:1, pl.ds(pl.multiple_of(block * width, width), width)]
            scaled[h, block] = (total[b * ROWS:(b + 1) * ROWS] * factor).astype(scaled.dtype)
        gather_beside(h, p).start()
        for i in range(1, cols):
            gather_z(h, p, i).start()
        hand_over(h, p).start()
    for h in range(parts):
        for i in range(1, cols):
            p = y * cols + zed(i)
            gather_z(h, p, i).wait_recv()
            gather_beside(h, p).start()
            hand_over(h, p).start()
    for h in range(parts):
        for i in range(cols):
            p = (1 - y) * cols + zed(i)
            gather_beside(h, p).wait_recv()
            hand_over(h, p).start()
    for h in range(parts):
        for p in range(chips):
            take_over(h, p).wait_recv()

    def back_step(i, carry):
        for j in range(STEP):
            s = i * STEP + j
            terms[lines(s, 1)] = lax.dot_general(
                jnp.concatenate([scaled[h, bobs[0, s]] for h in range(parts)], axis=0), blocks[s],
                (((1,), (1,)), ((), ())), preferred_element_type=jnp.float32)
        return carry

    lax.fori_loop(0, slots // STEP, back_step, 0)

    def exchange(i, slot, h):
        at = pl.ds(h * ROWS, ROWS)
        return remote(
            xsend.at[i - 1, at], xrecv.at[slot, at], sx.at[i - 1, h], rx.at[slot, h],
            {"grp": other(i)})

    for i in range(1, groups):
        chosen = chooser(bparam_row[...], other(i) * per, per)
        for h in range(parts):
            for k in range(ROWS):
                half_out[pl.ds(k, per, stride=ROWS), :] = summed(chosen, h * ROWS + k)
            for b in range(per):
                xsend[i - 1, h * ROWS:(h + 1) * ROWS, b * width:(b + 1) * width] = (
                    half_out[b * ROWS:(b + 1) * ROWS, :].astype(xsend.dtype))
            exchange(i, groups - i - 1, h).start()
    chosen = chooser(bparam_row[...], g * per, per)
    for h in range(parts):
        for k in range(ROWS):
            half_out[pl.ds(k, per, stride=ROWS), :] = summed(chosen, h * ROWS + k)
        for b in range(per):
            own_ref[h * ROWS:(h + 1) * ROWS, b * width:(b + 1) * width] = (
                half_out[b * ROWS:(b + 1) * ROWS, :])

    for h in range(parts):
        for r in range(rows):
            to_mate(h, r).wait_send()
        to_beside(h).wait_send()
        scale_to_beside(h).wait_send()
        for i in range(1, cols):
            to_z(h, i, z).wait_send()
            scale_to_z(h, i, z).wait_send()
            gather_z(h, y * cols + z, i).wait_send()
        for i in range(cols):
            gather_beside(h, y * cols + i).wait_send()
        for p in range(chips):
            hand_over(h, p).wait_send()
    for i in range(1, groups):
        for h in range(parts):
            exchange(i, groups - i - 1, h).wait_send()
            exchange(i, i - 1, h).wait_recv()


def on_device(groups, n, omega, blocks, bparam, bobs, count, weights):
    probes = omega.shape[0]
    slots, width = blocks.shape[1], blocks.shape[2]
    oblocks = weights.shape[1] // width
    pblocks = omega.shape[1] // width
    per = pblocks // groups
    chips = n // 2
    cols = chips // 2
    row = cols * (oblocks // n) * ROWS
    piece = oblocks // n * ROWS
    parts = probes // ROWS
    dma = pltpu.SemaphoreType.DMA
    hbm = pl.BlockSpec(memory_space=pl.ANY)
    vmem = pl.BlockSpec(memory_space=pltpu.VMEM)
    own, others = pl.pallas_call(
        functools.partial(kernel, n, groups),
        out_shape=(
            jax.ShapeDtypeStruct((probes, per * width), jnp.float32),
            jax.ShapeDtypeStruct((groups - 1, probes, per * width), jnp.bfloat16),
        ),
        in_specs=[hbm, hbm, pl.BlockSpec(memory_space=pltpu.SMEM), hbm, hbm, hbm],
        out_specs=(vmem, vmem),
        scratch_shapes=[
            pltpu.SMEM(bparam.shape, jnp.int32),
            pltpu.SMEM(bobs.shape, jnp.int32),
            pltpu.VMEM(bparam.shape, jnp.int32),
            pltpu.VMEM(bobs.shape, jnp.int32),
            pltpu.VMEM(omega.shape, omega.dtype),
            pltpu.VMEM((pblocks, probes, width), omega.dtype),
            pltpu.VMEM(weights.shape, weights.dtype),
            pltpu.VMEM(blocks.shape[1:], blocks.dtype),
            pltpu.VMEM((slots * probes, width), jnp.float32),
            pltpu.VMEM((oblocks * probes, width), jnp.float32),
            pltpu.VMEM((parts, oblocks, ROWS, width), jnp.bfloat16),
            pltpu.VMEM((parts, 2, row, width), jnp.float32),
            pltpu.VMEM((parts, row, width), jnp.int16),
            pltpu.VMEM((parts, row, width), jnp.int16),
            pltpu.VMEM((parts, 8, width), jnp.float32),
            pltpu.VMEM((parts, 8, width), jnp.float32),
            pltpu.VMEM((parts, cols, piece, width), jnp.int16),
            pltpu.VMEM((parts, cols, piece, width), jnp.int16),
            pltpu.VMEM((parts, 8, width), jnp.float32),
            pltpu.VMEM((parts, cols, 8, width), jnp.float32),
            pltpu.VMEM((per * ROWS, width), jnp.float32),
            pltpu.VMEM((groups - 1, probes, per * width), jnp.bfloat16),
            dma((6,)),
            dma((slots // STEP,)),
            dma((parts, 2)), dma((parts, 2)),
            dma((parts,)), dma((parts,)),
            dma((parts, cols)), dma((parts, chips)),
            dma((parts, chips)), dma((parts, chips)),
            dma((parts,)), dma((parts,)),
            dma((parts, chips)),
            dma((parts, cols)), dma((parts, cols)),
            dma((parts, cols)), dma((parts, cols)),
            dma((groups - 1, parts)), dma((groups - 1, parts)),
        ],
        compiler_params=pltpu.CompilerParams(
            collective_id=0, has_side_effects=True, vmem_limit_bytes=VMEM_LIMIT),
        cost_estimate=pl.CostEstimate(
            flops=4 * slots * probes * width * width,
            bytes_accessed=2 * slots * width * width, transcendentals=0),
    )(bparam, bobs, count, omega, blocks, weights)
    return own + jnp.sum(others.astype(jnp.float32), axis=0)


def solution(mesh):
    in_specs = (
        P(None, "par"),
        P("grp", "par", None, None),
        P("grp", "par"),
        P("grp", "par"),
        P("grp", "par"),
        P("grp", None),
    )
    out_specs = P(None, ("par", "grp"))
    body = functools.partial(on_device, mesh.shape["grp"], mesh.shape["par"])
    return jax.shard_map(
        body, mesh=mesh, in_specs=in_specs, out_specs=out_specs, check_vma=False
    )
```

```python
import functools

import jax
import jax.numpy as jnp
from jax import lax
from jax.experimental import pallas as pl
from jax.experimental.pallas import tpu as pltpu
from jax.sharding import PartitionSpec as P

MESH = pl.DeviceIdType.MESH
STEP = 16
ROWS = 16
WIDE = 4
LEVELS = 32000.0
VMEM_LIMIT = 57 * 1024 * 1024


def kernel(
    n, groups,
    bparam_hbm, bobs_hbm, count, omega_hbm, blocks_hbm, weight_hbm, own_ref, xrecv,
    bparam, bobs, bparam_row, bobs_row, omega, panels, weight, blocks,
    terms, split, part, scaled, sib, sbuf, rbuf, sscale, rscale, zsbuf, zrbuf, zsscale, zrscale,
    half_out, own, xsend,
    small, big, s1, r1, s2, r2, s3, r3, s4, r4, s5, r5, s6, s7, r7, s8, r8, sx, rx, so,
):
    me = lax.axis_index("par")
    g = lax.axis_index("grp")
    probes = omega.shape[0]
    slots, width = blocks.shape[0], blocks.shape[1]
    oblocks = weight.shape[1] // width
    pblocks = omega.shape[1] // width
    per = pblocks // groups
    chips = n // 2
    rows = 2
    cols = chips // rows
    q, c = me // 2, lax.rem(me, 2)
    z, y = q // rows, lax.rem(q, rows)
    half = oblocks // 2
    nb = half // chips
    mate = {"par": 2 * q + 1 - c}
    beside = {"par": 2 * (rows * z + 1 - y) + c}

    parts = probes // ROWS

    def zed(i):
        return lax.rem(z + i, cols)

    def at_z(i):
        return {"par": 2 * (rows * zed(i) + y) + c}

    def other(i):
        return lax.rem(g + i, groups)

    def lines(block, length):
        return pl.ds(pl.multiple_of(block * probes, probes), length * probes)

    def part_lines(h, block, length):
        at = (h * oblocks + block) * ROWS
        return pl.ds(pl.multiple_of(at, ROWS), length * ROWS)

    def mine(p):
        return pl.ds(c * half + p * nb, nb)

    def theirs(p):
        return pl.ds((1 - c) * half + p * nb, nb)

    early = [
        pltpu.make_async_copy(bparam_hbm, bparam, small.at[0]),
        pltpu.make_async_copy(bobs_hbm, bobs, small.at[1]),
        pltpu.make_async_copy(omega_hbm, omega, small.at[2]),
        pltpu.make_async_copy(bparam_hbm, bparam_row, small.at[3]),
        pltpu.make_async_copy(bobs_hbm, bobs_row, small.at[4]),
        pltpu.make_async_copy(weight_hbm, weight, small.at[5]),
    ]

    def blocks_of(i):
        at = pl.ds(i * STEP, STEP)
        return pltpu.make_async_copy(blocks_hbm.at[0, at], blocks.at[at], big.at[i])

    for copy in early:
        copy.start()
    for i in range(slots // STEP):
        blocks_of(i).start()

    barrier = pltpu.get_barrier_semaphore()
    pl.semaphore_signal(barrier, inc=1, device_id=mate, device_id_type=MESH)
    pl.semaphore_signal(barrier, inc=1, device_id=beside, device_id_type=MESH)
    for i in range(1, cols):
        pl.semaphore_signal(barrier, inc=1, device_id=at_z(i), device_id_type=MESH)
    for i in range(1, groups):
        pl.semaphore_signal(barrier, inc=1, device_id={"grp": other(i)}, device_id_type=MESH)

    for copy in early:
        copy.wait()
    for b in range(pblocks):
        panels[b] = omega[:, b * width:(b + 1) * width]

    def fwd_step(i, carry):
        blocks_of(i).wait()
        for j in range(STEP):
            s = i * STEP + j
            terms[lines(s, 1)] = jnp.dot(
                panels[bparam[0, s]], blocks[s], preferred_element_type=jnp.float32)
        return carry

    lax.fori_loop(0, slots // STEP, fwd_step, 0)

    used = lax.broadcasted_iota(jnp.int32, (1, slots), 1) < count[0, 0]

    def chooser(row, first, length):
        place = lax.broadcasted_iota(jnp.int32, (length, slots), 0) + first
        chosen = jnp.where((place == row) & used, 1.0, 0.0).astype(jnp.bfloat16)
        return jnp.concatenate([chosen, chosen], axis=1)

    def spread(h):
        for k in range(h * ROWS, (h + 1) * ROWS):
            value = terms[pl.ds(k, slots, stride=probes), :]
            high = value.astype(jnp.bfloat16)
            split[0:slots, k * width:(k + 1) * width] = high
            split[slots:, k * width:(k + 1) * width] = (
                value - high.astype(jnp.float32)).astype(jnp.bfloat16)

    def summed(chosen, k):
        return jnp.dot(
            chosen, split[:, k * width:(k + WIDE) * width], preferred_element_type=jnp.float32)

    def remote(src, dst, send, recv, device):
        return pltpu.make_async_remote_copy(
            src_ref=src, dst_ref=dst, send_sem=send, recv_sem=recv,
            device_id=device, device_id_type=MESH)

    row_blocks = cols * nb

    def to_mate(h, r):
        return remote(
            part.at[part_lines(h, (1 - c) * half + r * row_blocks, row_blocks)],
            sib.at[h, r], s1.at[h, r], r1.at[h, r], mate)

    def to_beside(h):
        return remote(sbuf.at[h], rbuf.at[h], s2.at[h], r2.at[h], beside)

    def scale_to_beside(h):
        return remote(sscale.at[h], rscale.at[h], s5.at[h], r5.at[h], beside)

    def to_z(h, i, lands):
        return remote(
            zsbuf.at[h, zed(i)], zrbuf.at[h, lands], s7.at[h, zed(i)], r7.at[h, lands], at_z(i))

    def scale_to_z(h, i, lands):
        return remote(zsscale.at[h], zrscale.at[h, lands], s8.at[h, zed(i)], r8.at[h, lands], at_z(i))

    def gather_z(h, p, i):
        piece = scaled.at[h, mine(p)]
        return remote(piece, piece, s3.at[h, zed(i)], r3.at[h, p], at_z(i))

    def gather_beside(h, p):
        piece = scaled.at[h, mine(p)]
        return remote(piece, piece, s6.at[h, p], r3.at[h, p], beside)

    def hand_over(h, p):
        piece = scaled.at[h, mine(p)]
        return remote(piece, piece, s4.at[h, p], r4.at[h, p], mate)

    def take_over(h, p):
        piece = scaled.at[h, theirs(p)]
        return remote(piece, piece, s4.at[h, p], r4.at[h, p], mate)

    def coded(value):
        largest = jnp.maximum(jnp.max(jnp.abs(value), axis=0, keepdims=True), 1e-30)
        level = jnp.round(value * (LEVELS / largest)).astype(jnp.int32).astype(jnp.int16)
        return level, jnp.broadcast_to(largest * (1.0 / LEVELS), (8, width))

    def decoded(level, scale):
        return level.astype(jnp.int32).astype(jnp.float32) * scale[0:1]

    def row_sum(h, r):
        to_mate(h, r).wait_recv()
        return part[part_lines(h, c * half + r * row_blocks, row_blocks), :] + sib[h, r]

    by_obs = chooser(bobs_row[...], 0, oblocks)
    for h in range(parts):
        spread(h)
        for k in range(0, ROWS, WIDE):
            value = summed(by_obs, h * ROWS + k)
            for j in range(WIDE):
                part[pl.ds(h * oblocks * ROWS + k + j, oblocks, stride=ROWS), :] = (
                    value[:, j * width:(j + 1) * width])
        if h == 0:
            pl.semaphore_wait(barrier, cols + groups)
        to_mate(h, 1 - y).start()
        to_mate(h, y).start()
    for h in range(parts):
        level, scale = coded(row_sum(h, 1 - y))
        sscale[h] = scale
        scale_to_beside(h).start()
        sbuf[h] = level
        to_beside(h).start()
    totals = []
    for h in range(parts):
        value = row_sum(h, y)
        scale_to_beside(h).wait_recv()
        to_beside(h).wait_recv()
        value += decoded(rbuf[h], rscale[h])
        level, scale = coded(value)
        zsscale[h] = scale
        piece = nb * ROWS
        for j in range(cols):
            zsbuf[h, j] = level[j * piece:(j + 1) * piece]
        sib[h, y] = value
        for i in range(1, cols):
            scale_to_z(h, i, z).start()
            to_z(h, i, z).start()
    for h in range(parts):
        at = pl.ds(pl.multiple_of(z * piece, piece), piece)
        total = sib[h, y, at, :]
        for i in range(1, cols):
            scale_to_z(h, i, zed(i)).wait_recv()
            to_z(h, i, zed(i)).wait_recv()
            total += decoded(zrbuf[h, zed(i)], zrscale[h, zed(i)])
        p = y * cols + z
        for b in range(nb):
            block = c * half + p * nb + b
            factor = weight[0:1, pl.ds(pl.multiple_of(block * width, width), width)]
            scaled[h, block] = (total[b * ROWS:(b + 1) * ROWS] * factor).astype(scaled.dtype)
        gather_beside(h, p).start()
        for i in range(1, cols):
            gather_z(h, p, i).start()
        hand_over(h, p).start()
    for h in range(parts):
        for i in range(1, cols):
            p = y * cols + zed(i)
            gather_z(h, p, i).wait_recv()
            gather_beside(h, p).start()
            hand_over(h, p).start()
    for h in range(parts):
        for i in range(cols):
            p = (1 - y) * cols + zed(i)
            gather_beside(h, p).wait_recv()
            hand_over(h, p).start()
    for h in range(parts):
        for p in range(chips):
            take_over(h, p).wait_recv()

    def back_step(i, carry):
        for j in range(STEP):
            s = i * STEP + j
            terms[lines(s, 1)] = lax.dot_general(
                jnp.concatenate([scaled[h, bobs[0, s]] for h in range(parts)], axis=0), blocks[s],
                (((1,), (1,)), ((), ())), preferred_element_type=jnp.float32)
        return carry

    lax.fori_loop(0, slots // STEP, back_step, 0)

    def keep(h):
        at = pl.ds(h * ROWS, ROWS)
        return pltpu.make_async_copy(own.at[at], own_ref.at[at], so.at[h])

    def exchange(i, slot, h):
        at = pl.ds(h * ROWS, ROWS)
        return remote(
            xsend.at[i - 1, at], xrecv.at[slot, at], sx.at[i - 1, h], rx.at[slot, h],
            {"grp": other(i)})

    def placed(chosen, h):
        for k in range(0, ROWS, WIDE):
            value = summed(chosen, h * ROWS + k)
            for j in range(WIDE):
                half_out[pl.ds(k + j, per, stride=ROWS), :] = value[:, j * width:(j + 1) * width]

    for i in range(1, groups):
        chosen = chooser(bparam_row[...], other(i) * per, per)
        for h in range(parts):
            if i == 1:
                spread(h)
            placed(chosen, h)
            for b in range(per):
                xsend[i - 1, h * ROWS:(h + 1) * ROWS, b * width:(b + 1) * width] = (
                    half_out[b * ROWS:(b + 1) * ROWS, :].astype(xsend.dtype))
            exchange(i, groups - i - 1, h).start()
    chosen = chooser(bparam_row[...], g * per, per)
    for h in range(parts):
        placed(chosen, h)
        for b in range(per):
            own[h * ROWS:(h + 1) * ROWS, b * width:(b + 1) * width] = (
                half_out[b * ROWS:(b + 1) * ROWS, :])
        keep(h).start()

    for h in range(parts):
        for r in range(rows):
            to_mate(h, r).wait_send()
        to_beside(h).wait_send()
        scale_to_beside(h).wait_send()
        for i in range(1, cols):
            to_z(h, i, z).wait_send()
            scale_to_z(h, i, z).wait_send()
            gather_z(h, y * cols + z, i).wait_send()
        for i in range(cols):
            gather_beside(h, y * cols + i).wait_send()
        for p in range(chips):
            hand_over(h, p).wait_send()
    for i in range(1, groups):
        for h in range(parts):
            exchange(i, groups - i - 1, h).wait_send()
            exchange(i, i - 1, h).wait_recv()
    for h in range(parts):
        keep(h).wait()


def on_device(groups, n, omega, blocks, bparam, bobs, count, weights):
    probes = omega.shape[0]
    slots, width = blocks.shape[1], blocks.shape[2]
    oblocks = weights.shape[1] // width
    pblocks = omega.shape[1] // width
    per = pblocks // groups
    chips = n // 2
    cols = chips // 2
    row = cols * (oblocks // n) * ROWS
    piece = oblocks // n * ROWS
    parts = probes // ROWS
    dma = pltpu.SemaphoreType.DMA
    hbm = pl.BlockSpec(memory_space=pl.ANY)
    own, others = pl.pallas_call(
        functools.partial(kernel, n, groups),
        out_shape=(
            jax.ShapeDtypeStruct((probes, per * width), jnp.float32),
            jax.ShapeDtypeStruct((groups - 1, probes, per * width), jnp.bfloat16),
        ),
        in_specs=[hbm, hbm, pl.BlockSpec(memory_space=pltpu.SMEM), hbm, hbm, hbm],
        out_specs=(hbm, hbm),
        scratch_shapes=[
            pltpu.SMEM(bparam.shape, jnp.int32),
            pltpu.SMEM(bobs.shape, jnp.int32),
            pltpu.VMEM(bparam.shape, jnp.int32),
            pltpu.VMEM(bobs.shape, jnp.int32),
            pltpu.VMEM(omega.shape, omega.dtype),
            pltpu.VMEM((pblocks, probes, width), omega.dtype),
            pltpu.VMEM(weights.shape, weights.dtype),
            pltpu.VMEM(blocks.shape[1:], blocks.dtype),
            pltpu.VMEM((slots * probes, width), jnp.float32),
            pltpu.VMEM((2 * slots, probes * width), jnp.bfloat16),
            pltpu.VMEM((oblocks * probes, width), jnp.float32),
            pltpu.VMEM((parts, oblocks, ROWS, width), jnp.bfloat16),
            pltpu.VMEM((parts, 2, row, width), jnp.float32),
            pltpu.VMEM((parts, row, width), jnp.int16),
            pltpu.VMEM((parts, row, width), jnp.int16),
            pltpu.VMEM((parts, 8, width), jnp.float32),
            pltpu.VMEM((parts, 8, width), jnp.float32),
            pltpu.VMEM((parts, cols, piece, width), jnp.int16),
            pltpu.VMEM((parts, cols, piece, width), jnp.int16),
            pltpu.VMEM((parts, 8, width), jnp.float32),
            pltpu.VMEM((parts, cols, 8, width), jnp.float32),
            pltpu.VMEM((per * ROWS, width), jnp.float32),
            pltpu.VMEM((probes, per * width), jnp.float32),
            pltpu.VMEM((groups - 1, probes, per * width), jnp.bfloat16),
            dma((6,)),
            dma((slots // STEP,)),
            dma((parts, 2)), dma((parts, 2)),
            dma((parts,)), dma((parts,)),
            dma((parts, cols)), dma((parts, chips)),
            dma((parts, chips)), dma((parts, chips)),
            dma((parts,)), dma((parts,)),
            dma((parts, chips)),
            dma((parts, cols)), dma((parts, cols)),
            dma((parts, cols)), dma((parts, cols)),
            dma((groups - 1, parts)), dma((groups - 1, parts)), dma((parts,)),
        ],
        compiler_params=pltpu.CompilerParams(
            collective_id=0, has_side_effects=True, vmem_limit_bytes=VMEM_LIMIT),
        cost_estimate=pl.CostEstimate(
            flops=4 * slots * probes * width * width,
            bytes_accessed=2 * slots * width * width, transcendentals=0),
    )(bparam, bobs, count, omega, blocks, weights)
    return own + jnp.sum(others.astype(jnp.float32), axis=0)


def solution(mesh):
    in_specs = (
        P(None, "par"),
        P("grp", "par", None, None),
        P("grp", "par"),
        P("grp", "par"),
        P("grp", "par"),
        P("grp", None),
    )
    out_specs = P(None, ("par", "grp"))
    body = functools.partial(on_device, mesh.shape["grp"], mesh.shape["par"])
    return jax.shard_map(
        body, mesh=mesh, in_specs=in_specs, out_specs=out_specs, check_vma=False
    )
```

```python
import functools

import jax
import jax.numpy as jnp
from jax import lax
from jax.experimental import pallas as pl
from jax.experimental.pallas import tpu as pltpu
from jax.sharding import PartitionSpec as P

MESH = pl.DeviceIdType.MESH
STEP = 16
ROWS = 16
TAIL = 16
WIDE = 4
LEVELS = 32000.0
VMEM_LIMIT = 57 * 1024 * 1024


def kernel(
    n, groups,
    bparam_hbm, bobs_hbm, count, omega_hbm, blocks_hbm, weight_hbm, own_ref, xrecv,
    bparam, bobs, bparam_row, bobs_row, omega, panels, weight, blocks,
    terms, split, part, scaled, sib, sbuf, rbuf, zsbuf, zrbuf,
    half_out, own, xsend,
    small, big, s1, r1, s2, r2, s3, r3, s4, r4, s6, r6, s7, r7, sx, rx, so,
):
    me = lax.axis_index("par")
    g = lax.axis_index("grp")
    probes = omega.shape[0]
    slots, width = blocks.shape[0], blocks.shape[1]
    oblocks = weight.shape[1] // width
    pblocks = omega.shape[1] // width
    per = pblocks // groups
    chips = n // 2
    rows = 2
    cols = chips // rows
    q, c = me // 2, lax.rem(me, 2)
    z, y = q // rows, lax.rem(q, rows)
    half = oblocks // 2
    nb = half // chips
    mate = {"par": 2 * q + 1 - c}
    beside = {"par": 2 * (rows * z + 1 - y) + c}

    parts = probes // ROWS

    def zed(i):
        return lax.rem(z + i, cols)

    def at_z(i):
        return {"par": 2 * (rows * zed(i) + y) + c}

    def other(i):
        return lax.rem(g + i, groups)

    def lines(block, length):
        return pl.ds(pl.multiple_of(block * probes, probes), length * probes)

    def part_lines(h, block, length):
        at = (h * oblocks + block) * ROWS
        return pl.ds(pl.multiple_of(at, ROWS), length * ROWS)

    def mine(p):
        return pl.ds(c * half + p * nb, nb)

    early = [
        pltpu.make_async_copy(bparam_hbm, bparam, small.at[0]),
        pltpu.make_async_copy(bobs_hbm, bobs, small.at[1]),
        pltpu.make_async_copy(omega_hbm, omega, small.at[2]),
        pltpu.make_async_copy(bparam_hbm, bparam_row, small.at[3]),
        pltpu.make_async_copy(bobs_hbm, bobs_row, small.at[4]),
        pltpu.make_async_copy(weight_hbm, weight, small.at[5]),
    ]

    def blocks_of(i):
        at = pl.ds(i * STEP, STEP)
        return pltpu.make_async_copy(blocks_hbm.at[0, at], blocks.at[at], big.at[i])

    for copy in early:
        copy.start()
    for i in range(slots // STEP):
        blocks_of(i).start()

    barrier = pltpu.get_barrier_semaphore()
    pl.semaphore_signal(barrier, inc=1, device_id=mate, device_id_type=MESH)
    pl.semaphore_signal(barrier, inc=1, device_id=beside, device_id_type=MESH)
    for i in range(1, cols):
        pl.semaphore_signal(barrier, inc=1, device_id=at_z(i), device_id_type=MESH)
    for i in range(1, groups):
        pl.semaphore_signal(barrier, inc=1, device_id={"grp": other(i)}, device_id_type=MESH)

    for copy in early:
        copy.wait()
    for b in range(pblocks):
        panels[b] = omega[:, b * width:(b + 1) * width]

    def fwd_step(i, carry):
        blocks_of(i).wait()
        for j in range(STEP):
            s = i * STEP + j
            terms[lines(s, 1)] = jnp.dot(
                panels[bparam[0, s]], blocks[s], preferred_element_type=jnp.float32)
        return carry

    lax.fori_loop(0, slots // STEP, fwd_step, 0)

    used = lax.broadcasted_iota(jnp.int32, (1, slots), 1) < count[0, 0]

    def chooser(row, first, length):
        place = lax.broadcasted_iota(jnp.int32, (length, slots), 0) + first
        chosen = jnp.where((place == row) & used, 1.0, 0.0).astype(jnp.bfloat16)
        return jnp.concatenate([chosen, chosen], axis=1)

    def spread(h):
        for k in range(h * ROWS, (h + 1) * ROWS):
            value = terms[pl.ds(k, slots, stride=probes), :]
            high = value.astype(jnp.bfloat16)
            split[0:slots, k * width:(k + 1) * width] = high
            split[slots:, k * width:(k + 1) * width] = (
                value - high.astype(jnp.float32)).astype(jnp.bfloat16)

    def summed(chosen, k):
        return jnp.dot(
            chosen, split[:, k * width:(k + WIDE) * width], preferred_element_type=jnp.float32)

    def remote(src, dst, send, recv, device):
        return pltpu.make_async_remote_copy(
            src_ref=src, dst_ref=dst, send_sem=send, recv_sem=recv,
            device_id=device, device_id_type=MESH)

    row_blocks = cols * nb

    def to_mate(h, r):
        return remote(
            part.at[part_lines(h, (1 - c) * half + r * row_blocks, row_blocks)],
            sib.at[h, r], s1.at[h, r], r1.at[h, r], mate)

    def to_beside(h):
        return remote(sbuf.at[h], rbuf.at[h], s2.at[h], r2.at[h], beside)

    def to_z(h, i, lands):
        return remote(
            zsbuf.at[h, zed(i)], zrbuf.at[h, lands], s7.at[h, zed(i)], r7.at[h, lands], at_z(i))

    def gather_z(h, p, i):
        piece = scaled.at[h, mine(p)]
        return remote(piece, piece, s3.at[h, zed(i)], r3.at[h, p], at_z(i))

    def row_of(core, r):
        return pl.ds(core * half + r * row_blocks, row_blocks)

    def gather_beside(h, r):
        piece = scaled.at[h, row_of(c, r)]
        return remote(piece, piece, s6.at[h], r6.at[h], beside)

    def hand_over(h, core, r):
        piece = scaled.at[h, row_of(core, r)]
        return remote(piece, piece, s4.at[h, r], r4.at[h, r], mate)

    def coded(value):
        largest = jnp.maximum(jnp.max(jnp.abs(value), axis=0, keepdims=True), 1e-30)
        power = jnp.ceil(jnp.log2(largest))
        level = jnp.round(value * (jnp.exp2(-power) * LEVELS)).astype(jnp.int32)
        tail = jnp.broadcast_to(power.astype(jnp.int32), (TAIL, width))
        return level.astype(jnp.int16), tail.astype(jnp.int16)

    def decoded(message):
        value = message.astype(jnp.int32).astype(jnp.float32)
        size = value.shape[0] - TAIL
        return value[:size] * (jnp.exp2(value[size:size + 1]) * (1.0 / LEVELS))

    def row_sum(h, r):
        to_mate(h, r).wait_recv()
        return part[part_lines(h, c * half + r * row_blocks, row_blocks), :] + sib[h, r]

    by_obs = chooser(bobs_row[...], 0, oblocks)
    for h in range(parts):
        spread(h)
        for k in range(0, ROWS, WIDE):
            value = summed(by_obs, h * ROWS + k)
            for j in range(WIDE):
                part[pl.ds(h * oblocks * ROWS + k + j, oblocks, stride=ROWS), :] = (
                    value[:, j * width:(j + 1) * width])
        if h == 0:
            pl.semaphore_wait(barrier, cols + groups)
        to_mate(h, 1 - y).start()
        to_mate(h, y).start()
    for h in range(parts):
        level, tail = coded(row_sum(h, 1 - y))
        sbuf[h, 0:level.shape[0]] = level
        sbuf[h, level.shape[0]:] = tail
        to_beside(h).start()
    for h in range(parts):
        value = row_sum(h, y)
        to_beside(h).wait_recv()
        value += decoded(rbuf[h])
        level, tail = coded(value)
        piece = nb * ROWS
        for j in range(cols):
            zsbuf[h, j, 0:piece] = level[j * piece:(j + 1) * piece]
            zsbuf[h, j, piece:] = tail
        sib[h, y] = value
        for i in range(1, cols):
            to_z(h, i, z).start()
    for h in range(parts):
        at = pl.ds(pl.multiple_of(z * piece, piece), piece)
        total = sib[h, y, at, :]
        for i in range(1, cols):
            to_z(h, i, zed(i)).wait_recv()
            total += decoded(zrbuf[h, zed(i)])
        p = y * cols + z
        for b in range(nb):
            block = c * half + p * nb + b
            factor = weight[0:1, pl.ds(pl.multiple_of(block * width, width), width)]
            scaled[h, block] = (total[b * ROWS:(b + 1) * ROWS] * factor).astype(scaled.dtype)
        for i in range(1, cols):
            gather_z(h, p, i).start()
    for h in range(parts):
        for i in range(1, cols):
            gather_z(h, y * cols + zed(i), i).wait_recv()
        gather_beside(h, y).start()
        hand_over(h, c, y).start()
    for h in range(parts):
        gather_beside(h, 1 - y).wait_recv()
        hand_over(h, c, 1 - y).start()
    for h in range(parts):
        for r in range(rows):
            hand_over(h, 1 - c, r).wait_recv()

    def back_step(i, carry):
        for j in range(STEP):
            s = i * STEP + j
            terms[lines(s, 1)] = lax.dot_general(
                jnp.concatenate([scaled[h, bobs[0, s]] for h in range(parts)], axis=0), blocks[s],
                (((1,), (1,)), ((), ())), preferred_element_type=jnp.float32)
        return carry

    lax.fori_loop(0, slots // STEP, back_step, 0)

    def keep(h):
        at = pl.ds(h * ROWS, ROWS)
        return pltpu.make_async_copy(own.at[at], own_ref.at[at], so.at[h])

    def exchange(i, slot, h):
        at = pl.ds(h * ROWS, ROWS)
        return remote(
            xsend.at[i - 1, at], xrecv.at[slot, at], sx.at[i - 1, h], rx.at[slot, h],
            {"grp": other(i)})

    def placed(chosen, h):
        for k in range(0, ROWS, WIDE):
            value = summed(chosen, h * ROWS + k)
            for j in range(WIDE):
                half_out[pl.ds(k + j, per, stride=ROWS), :] = value[:, j * width:(j + 1) * width]

    for i in range(1, groups):
        chosen = chooser(bparam_row[...], other(i) * per, per)
        for h in range(parts):
            if i == 1:
                spread(h)
            placed(chosen, h)
            for b in range(per):
                xsend[i - 1, h * ROWS:(h + 1) * ROWS, b * width:(b + 1) * width] = (
                    half_out[b * ROWS:(b + 1) * ROWS, :].astype(xsend.dtype))
            exchange(i, groups - i - 1, h).start()
    chosen = chooser(bparam_row[...], g * per, per)
    for h in range(parts):
        placed(chosen, h)
        for b in range(per):
            own[h * ROWS:(h + 1) * ROWS, b * width:(b + 1) * width] = (
                half_out[b * ROWS:(b + 1) * ROWS, :])
        keep(h).start()

    for h in range(parts):
        for r in range(rows):
            to_mate(h, r).wait_send()
        to_beside(h).wait_send()
        gather_beside(h, y).wait_send()
        for i in range(1, cols):
            to_z(h, i, z).wait_send()
            gather_z(h, y * cols + z, i).wait_send()
        for r in range(rows):
            hand_over(h, c, r).wait_send()
    for i in range(1, groups):
        for h in range(parts):
            exchange(i, groups - i - 1, h).wait_send()
            exchange(i, i - 1, h).wait_recv()
    for h in range(parts):
        keep(h).wait()


def on_device(groups, n, omega, blocks, bparam, bobs, count, weights):
    probes = omega.shape[0]
    slots, width = blocks.shape[1], blocks.shape[2]
    oblocks = weights.shape[1] // width
    pblocks = omega.shape[1] // width
    per = pblocks // groups
    chips = n // 2
    cols = chips // 2
    row = cols * (oblocks // n) * ROWS
    piece = oblocks // n * ROWS
    parts = probes // ROWS
    dma = pltpu.SemaphoreType.DMA
    hbm = pl.BlockSpec(memory_space=pl.ANY)
    own, others = pl.pallas_call(
        functools.partial(kernel, n, groups),
        out_shape=(
            jax.ShapeDtypeStruct((probes, per * width), jnp.float32),
            jax.ShapeDtypeStruct((groups - 1, probes, per * width), jnp.bfloat16),
        ),
        in_specs=[hbm, hbm, pl.BlockSpec(memory_space=pltpu.SMEM), hbm, hbm, hbm],
        out_specs=(hbm, hbm),
        scratch_shapes=[
            pltpu.SMEM(bparam.shape, jnp.int32),
            pltpu.SMEM(bobs.shape, jnp.int32),
            pltpu.VMEM(bparam.shape, jnp.int32),
            pltpu.VMEM(bobs.shape, jnp.int32),
            pltpu.VMEM(omega.shape, omega.dtype),
            pltpu.VMEM((pblocks, probes, width), omega.dtype),
            pltpu.VMEM(weights.shape, weights.dtype),
            pltpu.VMEM(blocks.shape[1:], blocks.dtype),
            pltpu.VMEM((slots * probes, width), jnp.float32),
            pltpu.VMEM((2 * slots, probes * width), jnp.bfloat16),
            pltpu.VMEM((oblocks * probes, width), jnp.float32),
            pltpu.VMEM((parts, oblocks, ROWS, width), jnp.bfloat16),
            pltpu.VMEM((parts, 2, row, width), jnp.float32),
            pltpu.VMEM((parts, row + TAIL, width), jnp.int16),
            pltpu.VMEM((parts, row + TAIL, width), jnp.int16),
            pltpu.VMEM((parts, cols, piece + TAIL, width), jnp.int16),
            pltpu.VMEM((parts, cols, piece + TAIL, width), jnp.int16),
            pltpu.VMEM((per * ROWS, width), jnp.float32),
            pltpu.VMEM((probes, per * width), jnp.float32),
            pltpu.VMEM((groups - 1, probes, per * width), jnp.bfloat16),
            dma((6,)),
            dma((slots // STEP,)),
            dma((parts, 2)), dma((parts, 2)),
            dma((parts,)), dma((parts,)),
            dma((parts, cols)), dma((parts, chips)),
            dma((parts, 2)), dma((parts, 2)),
            dma((parts,)), dma((parts,)),
            dma((parts, cols)), dma((parts, cols)),
            dma((groups - 1, parts)), dma((groups - 1, parts)), dma((parts,)),
        ],
        compiler_params=pltpu.CompilerParams(
            collective_id=0, has_side_effects=True, vmem_limit_bytes=VMEM_LIMIT),
        cost_estimate=pl.CostEstimate(
            flops=4 * slots * probes * width * width,
            bytes_accessed=2 * slots * width * width, transcendentals=0),
    )(bparam, bobs, count, omega, blocks, weights)
    return own + jnp.sum(others.astype(jnp.float32), axis=0)


def solution(mesh):
    in_specs = (
        P(None, "par"),
        P("grp", "par", None, None),
        P("grp", "par"),
        P("grp", "par"),
        P("grp", "par"),
        P("grp", None),
    )
    out_specs = P(None, ("par", "grp"))
    body = functools.partial(on_device, mesh.shape["grp"], mesh.shape["par"])
    return jax.shard_map(
        body, mesh=mesh, in_specs=in_specs, out_specs=out_specs, check_vma=False
    )
```

```python
import functools

import jax
import jax.numpy as jnp
from jax import lax
from jax.experimental import pallas as pl
from jax.experimental.pallas import tpu as pltpu
from jax.sharding import PartitionSpec as P

MESH = pl.DeviceIdType.MESH
STEP = 16
ROWS = 16
TAIL = 16
WIDE = 4
LEVELS = 32000.0
VMEM_LIMIT = 57 * 1024 * 1024


def kernel(
    n, groups,
    bparam_hbm, bobs_hbm, count, omega_hbm, blocks_hbm, weight_hbm, own_ref, xrecv,
    bparam, bobs, bparam_row, bobs_row, omega, panels, weight, blocks,
    terms, split, part, scaled, sib, msend, held, sbuf, rbuf, zsbuf, zrbuf,
    half_out, own, xsend,
    small, big, s1, r1, s2, r2, s3, r3, s4, r4, s6, r6, s7, r7, sx, rx, so,
):
    me = lax.axis_index("par")
    g = lax.axis_index("grp")
    probes = omega.shape[0]
    slots, width = blocks.shape[0], blocks.shape[1]
    oblocks = weight.shape[1] // width
    pblocks = omega.shape[1] // width
    per = pblocks // groups
    chips = n // 2
    rows = 2
    cols = chips // rows
    q, c = me // 2, lax.rem(me, 2)
    z, y = q // rows, lax.rem(q, rows)
    half = oblocks // 2
    nb = half // chips
    mate = {"par": 2 * q + 1 - c}
    beside = {"par": 2 * (rows * z + 1 - y) + c}

    parts = probes // ROWS

    def zed(i):
        return lax.rem(z + i, cols)

    def at_z(i):
        return {"par": 2 * (rows * zed(i) + y) + c}

    def other(i):
        return lax.rem(g + i, groups)

    def lines(block, length):
        return pl.ds(pl.multiple_of(block * probes, probes), length * probes)

    def part_lines(h, block, length):
        at = (h * oblocks + block) * ROWS
        return pl.ds(pl.multiple_of(at, ROWS), length * ROWS)

    def mine(p):
        return pl.ds(c * half + p * nb, nb)

    early = [
        pltpu.make_async_copy(bparam_hbm, bparam, small.at[0]),
        pltpu.make_async_copy(bobs_hbm, bobs, small.at[1]),
        pltpu.make_async_copy(omega_hbm, omega, small.at[2]),
        pltpu.make_async_copy(bparam_hbm, bparam_row, small.at[3]),
        pltpu.make_async_copy(bobs_hbm, bobs_row, small.at[4]),
        pltpu.make_async_copy(weight_hbm, weight, small.at[5]),
    ]

    def blocks_of(i):
        at = pl.ds(i * STEP, STEP)
        return pltpu.make_async_copy(blocks_hbm.at[0, at], blocks.at[at], big.at[i])

    for copy in early:
        copy.start()
    for i in range(slots // STEP):
        blocks_of(i).start()

    barrier = pltpu.get_barrier_semaphore()
    pl.semaphore_signal(barrier, inc=1, device_id=mate, device_id_type=MESH)
    pl.semaphore_signal(barrier, inc=1, device_id=beside, device_id_type=MESH)
    for i in range(1, cols):
        pl.semaphore_signal(barrier, inc=1, device_id=at_z(i), device_id_type=MESH)
    for i in range(1, groups):
        pl.semaphore_signal(barrier, inc=1, device_id={"grp": other(i)}, device_id_type=MESH)

    for copy in early:
        copy.wait()
    for b in range(pblocks):
        panels[b] = omega[:, b * width:(b + 1) * width]

    def fwd_step(i, carry):
        blocks_of(i).wait()
        for j in range(STEP):
            s = i * STEP + j
            terms[lines(s, 1)] = jnp.dot(
                panels[bparam[0, s]], blocks[s], preferred_element_type=jnp.float32)
        return carry

    lax.fori_loop(0, slots // STEP, fwd_step, 0)

    used = lax.broadcasted_iota(jnp.int32, (1, slots), 1) < count[0, 0]

    def chooser(row, first, length):
        place = lax.broadcasted_iota(jnp.int32, (length, slots), 0) + first
        chosen = jnp.where((place == row) & used, 1.0, 0.0).astype(jnp.bfloat16)
        return jnp.concatenate([chosen, chosen], axis=1)

    def spread(h):
        for k in range(h * ROWS, (h + 1) * ROWS):
            value = terms[pl.ds(k, slots, stride=probes), :]
            high = value.astype(jnp.bfloat16)
            split[0:slots, k * width:(k + 1) * width] = high
            split[slots:, k * width:(k + 1) * width] = (
                value - high.astype(jnp.float32)).astype(jnp.bfloat16)

    def summed(chosen, k):
        return jnp.dot(
            chosen, split[:, k * width:(k + WIDE) * width], preferred_element_type=jnp.float32)

    def remote(src, dst, send, recv, device):
        return pltpu.make_async_remote_copy(
            src_ref=src, dst_ref=dst, send_sem=send, recv_sem=recv,
            device_id=device, device_id_type=MESH)

    row_blocks = cols * nb

    def to_mate(h, r):
        return remote(
            msend.at[h, r], sib.at[h, r], s1.at[h, r], r1.at[h, r], mate)

    def to_beside(h):
        return remote(sbuf.at[h], rbuf.at[h], s2.at[h], r2.at[h], beside)

    def to_z(h, i, lands):
        return remote(
            zsbuf.at[h, zed(i)], zrbuf.at[h, lands], s7.at[h, zed(i)], r7.at[h, lands], at_z(i))

    def gather_z(h, p, i):
        piece = scaled.at[h, mine(p)]
        return remote(piece, piece, s3.at[h, zed(i)], r3.at[h, p], at_z(i))

    def row_of(core, r):
        return pl.ds(core * half + r * row_blocks, row_blocks)

    def gather_beside(h, r):
        piece = scaled.at[h, row_of(c, r)]
        return remote(piece, piece, s6.at[h], r6.at[h], beside)

    def hand_over(h, core, r):
        piece = scaled.at[h, row_of(core, r)]
        return remote(piece, piece, s4.at[h, r], r4.at[h, r], mate)

    def coded(value):
        largest = jnp.maximum(jnp.max(jnp.abs(value), axis=0, keepdims=True), 1e-30)
        power = jnp.ceil(jnp.log2(largest))
        level = jnp.round(value * (jnp.exp2(-power) * LEVELS)).astype(jnp.int32)
        tail = jnp.broadcast_to(power.astype(jnp.int32), (TAIL, width))
        return level.astype(jnp.int16), tail.astype(jnp.int16)

    def decoded(message):
        value = message.astype(jnp.int32).astype(jnp.float32)
        size = value.shape[0] - TAIL
        return value[:size] * (jnp.exp2(value[size:size + 1]) * (1.0 / LEVELS))

    def row_sum(h, r):
        to_mate(h, r).wait_recv()
        return part[part_lines(h, c * half + r * row_blocks, row_blocks), :] + decoded(sib[h, r])

    by_obs = chooser(bobs_row[...], 0, oblocks)
    for h in range(parts):
        spread(h)
        for k in range(0, ROWS, WIDE):
            value = summed(by_obs, h * ROWS + k)
            for j in range(WIDE):
                part[pl.ds(h * oblocks * ROWS + k + j, oblocks, stride=ROWS), :] = (
                    value[:, j * width:(j + 1) * width])
        if h == 0:
            pl.semaphore_wait(barrier, cols + groups)
        for r in (1 - y, y):
            level, tail = coded(part[part_lines(h, (1 - c) * half + r * row_blocks, row_blocks), :])
            msend[h, r, 0:level.shape[0]] = level
            msend[h, r, level.shape[0]:] = tail
            to_mate(h, r).start()
    for h in range(parts):
        level, tail = coded(row_sum(h, 1 - y))
        sbuf[h, 0:level.shape[0]] = level
        sbuf[h, level.shape[0]:] = tail
        to_beside(h).start()
    for h in range(parts):
        value = row_sum(h, y)
        to_beside(h).wait_recv()
        value += decoded(rbuf[h])
        level, tail = coded(value)
        piece = nb * ROWS
        for j in range(cols):
            zsbuf[h, j, 0:piece] = level[j * piece:(j + 1) * piece]
            zsbuf[h, j, piece:] = tail
        held[h] = value
        for i in range(1, cols):
            to_z(h, i, z).start()
    for h in range(parts):
        at = pl.ds(pl.multiple_of(z * piece, piece), piece)
        total = held[h, at, :]
        for i in range(1, cols):
            to_z(h, i, zed(i)).wait_recv()
            total += decoded(zrbuf[h, zed(i)])
        p = y * cols + z
        for b in range(nb):
            block = c * half + p * nb + b
            factor = weight[0:1, pl.ds(pl.multiple_of(block * width, width), width)]
            scaled[h, block] = (total[b * ROWS:(b + 1) * ROWS] * factor).astype(scaled.dtype)
        for i in range(1, cols):
            gather_z(h, p, i).start()
    for h in range(parts):
        for i in range(1, cols):
            gather_z(h, y * cols + zed(i), i).wait_recv()
        gather_beside(h, y).start()
        hand_over(h, c, y).start()
    for h in range(parts):
        gather_beside(h, 1 - y).wait_recv()
        hand_over(h, c, 1 - y).start()
    for h in range(parts):
        for r in range(rows):
            hand_over(h, 1 - c, r).wait_recv()

    def back_step(i, carry):
        for j in range(STEP):
            s = i * STEP + j
            terms[lines(s, 1)] = lax.dot_general(
                jnp.concatenate([scaled[h, bobs[0, s]] for h in range(parts)], axis=0), blocks[s],
                (((1,), (1,)), ((), ())), preferred_element_type=jnp.float32)
        return carry

    lax.fori_loop(0, slots // STEP, back_step, 0)

    def keep(h):
        at = pl.ds(h * ROWS, ROWS)
        return pltpu.make_async_copy(own.at[at], own_ref.at[at], so.at[h])

    def exchange(i, slot, h):
        at = pl.ds(h * ROWS, ROWS)
        return remote(
            xsend.at[i - 1, at], xrecv.at[slot, at], sx.at[i - 1, h], rx.at[slot, h],
            {"grp": other(i)})

    def placed(chosen, h):
        for k in range(0, ROWS, WIDE):
            value = summed(chosen, h * ROWS + k)
            for j in range(WIDE):
                half_out[pl.ds(k + j, per, stride=ROWS), :] = value[:, j * width:(j + 1) * width]

    for i in range(1, groups):
        chosen = chooser(bparam_row[...], other(i) * per, per)
        for h in range(parts):
            if i == 1:
                spread(h)
            placed(chosen, h)
            for b in range(per):
                xsend[i - 1, h * ROWS:(h + 1) * ROWS, b * width:(b + 1) * width] = (
                    half_out[b * ROWS:(b + 1) * ROWS, :].astype(xsend.dtype))
            exchange(i, groups - i - 1, h).start()
    chosen = chooser(bparam_row[...], g * per, per)
    for h in range(parts):
        placed(chosen, h)
        for b in range(per):
            own[h * ROWS:(h + 1) * ROWS, b * width:(b + 1) * width] = (
                half_out[b * ROWS:(b + 1) * ROWS, :])
        keep(h).start()

    for h in range(parts):
        for r in range(rows):
            to_mate(h, r).wait_send()
        to_beside(h).wait_send()
        gather_beside(h, y).wait_send()
        for i in range(1, cols):
            to_z(h, i, z).wait_send()
            gather_z(h, y * cols + z, i).wait_send()
        for r in range(rows):
            hand_over(h, c, r).wait_send()
    for i in range(1, groups):
        for h in range(parts):
            exchange(i, groups - i - 1, h).wait_send()
            exchange(i, i - 1, h).wait_recv()
    for h in range(parts):
        keep(h).wait()


def on_device(groups, n, omega, blocks, bparam, bobs, count, weights):
    probes = omega.shape[0]
    slots, width = blocks.shape[1], blocks.shape[2]
    oblocks = weights.shape[1] // width
    pblocks = omega.shape[1] // width
    per = pblocks // groups
    chips = n // 2
    cols = chips // 2
    row = cols * (oblocks // n) * ROWS
    piece = oblocks // n * ROWS
    parts = probes // ROWS
    dma = pltpu.SemaphoreType.DMA
    hbm = pl.BlockSpec(memory_space=pl.ANY)
    own, others = pl.pallas_call(
        functools.partial(kernel, n, groups),
        out_shape=(
            jax.ShapeDtypeStruct((probes, per * width), jnp.float32),
            jax.ShapeDtypeStruct((groups - 1, probes, per * width), jnp.bfloat16),
        ),
        in_specs=[hbm, hbm, pl.BlockSpec(memory_space=pltpu.SMEM), hbm, hbm, hbm],
        out_specs=(hbm, hbm),
        scratch_shapes=[
            pltpu.SMEM(bparam.shape, jnp.int32),
            pltpu.SMEM(bobs.shape, jnp.int32),
            pltpu.VMEM(bparam.shape, jnp.int32),
            pltpu.VMEM(bobs.shape, jnp.int32),
            pltpu.VMEM(omega.shape, omega.dtype),
            pltpu.VMEM((pblocks, probes, width), omega.dtype),
            pltpu.VMEM(weights.shape, weights.dtype),
            pltpu.VMEM(blocks.shape[1:], blocks.dtype),
            pltpu.VMEM((slots * probes, width), jnp.float32),
            pltpu.VMEM((2 * slots, probes * width), jnp.bfloat16),
            pltpu.VMEM((oblocks * probes, width), jnp.float32),
            pltpu.VMEM((parts, oblocks, ROWS, width), jnp.bfloat16),
            pltpu.VMEM((parts, 2, row + TAIL, width), jnp.int16),
            pltpu.VMEM((parts, 2, row + TAIL, width), jnp.int16),
            pltpu.VMEM((parts, row, width), jnp.float32),
            pltpu.VMEM((parts, row + TAIL, width), jnp.int16),
            pltpu.VMEM((parts, row + TAIL, width), jnp.int16),
            pltpu.VMEM((parts, cols, piece + TAIL, width), jnp.int16),
            pltpu.VMEM((parts, cols, piece + TAIL, width), jnp.int16),
            pltpu.VMEM((per * ROWS, width), jnp.float32),
            pltpu.VMEM((probes, per * width), jnp.float32),
            pltpu.VMEM((groups - 1, probes, per * width), jnp.bfloat16),
            dma((6,)),
            dma((slots // STEP,)),
            dma((parts, 2)), dma((parts, 2)),
            dma((parts,)), dma((parts,)),
            dma((parts, cols)), dma((parts, chips)),
            dma((parts, 2)), dma((parts, 2)),
            dma((parts,)), dma((parts,)),
            dma((parts, cols)), dma((parts, cols)),
            dma((groups - 1, parts)), dma((groups - 1, parts)), dma((parts,)),
        ],
        compiler_params=pltpu.CompilerParams(
            collective_id=0, has_side_effects=True, vmem_limit_bytes=VMEM_LIMIT),
        cost_estimate=pl.CostEstimate(
            flops=4 * slots * probes * width * width,
            bytes_accessed=2 * slots * width * width, transcendentals=0),
    )(bparam, bobs, count, omega, blocks, weights)
    return own + jnp.sum(others.astype(jnp.float32), axis=0)


def solution(mesh):
    in_specs = (
        P(None, "par"),
        P("grp", "par", None, None),
        P("grp", "par"),
        P("grp", "par"),
        P("grp", "par"),
        P("grp", None),
    )
    out_specs = P(None, ("par", "grp"))
    body = functools.partial(on_device, mesh.shape["grp"], mesh.shape["par"])
    return jax.shard_map(
        body, mesh=mesh, in_specs=in_specs, out_specs=out_specs, check_vma=False
    )
```
